256 devices in a mesh: pb: 16 (over x, y_lo, core), pa: 16 (over z, y_hi).
Axes of the slice: x: 4, y: 4 (y_hi: 2, y_lo: 2; y = y_hi * 2 + y_lo), z: 8, core: 2. Of those that a mesh axis runs over, the one named last changes fastest.
Arguments:
- queries: bfloat16 [4096, 128], P('pb'), may hold values from -10.5 to 10.5, as said below
- encoder_outputs: bfloat16 [16, 256, 128, 1024], P('pb', 'pa'), may hold values from -6 to 6
- proj_weight: bfloat16 [1024, 128], replicated, may hold values from -0.1875 to 0.1875
- bm25_rank: int32 [128, 16, 128], P('pb', 'pa'), may hold values from 0 to 199
- dense_rank: int32 [128, 16, 128], P('pb', 'pa'), may hold values from 0 to 199
- custodian_document_index: int32 [16, 256], P('pb', 'pa'), may hold values from -1 to 127, as said below
Outputs:
- query_grad: float32 [4096, 128], P(('pb', 'pa'))
- encoder_output_derivative: bfloat16 [16, 256, 128, 1024], P('pb', 'pa')
The draws below stay inside these ranges and needn't reach their ends.
Inputs may be any that keep to these rules, and one draw needn't show every extreme that they name: `queries`: A custom draw: each entry lies between the bounds; rows may differ in scale. `custodian_document_index`: within each row b every number n from 0 to 127 appears exactly once and stands for passage (n // 8, b * 8 + n % 8); all other entries are -1. The owner of columns o * 16 to o * 16 + 15 is index o of pa; an owner holds 0, 8 or 16 passages, and at most 1 with the same n // 8. Some owner is full and some owner holds exactly 1 passages with the same n // 8 in every row.
All inputs are finite; a program needn't handle non-finite values.
Results may differ from the reference program's by a relative error of at most 0.025.
The reference program's roundings to bfloat16 on the way count: a program that leaves them out, or rounds other values in their place, can miss the bound.
Values may be sent and summed in bfloat16 or wider, within the bound.
No kernel may reach another device: no remote copies, remote signals or barrier semaphores. Data moves between devices by JAX's collectives and lax.ppermute only.
A program may use at most 64 MiB of HBM per device.

```python
import jax
import jax.numpy as jnp
from jax import lax

DIM = 128
H = 1024
QT = 32
LEN = 128
PD = 8
DEPTH = 100
Q = 128
M = 128
CAP = 16
N_PB = 16
N_PA = 16


def draw_queries(key, part):
    shape = (Q * QT, DIM)
    values = 0.25 * jax.random.normal(key, shape, jnp.float32)
    return jnp.clip(values, -1.5, 1.5).astype(jnp.bfloat16)


def owner_group(key):
    order_key, slot_key = jax.random.split(jax.random.fold_in(key, 7))
    owner_order = jax.random.permutation(order_key, N_PA)
    owner_rank = jnp.argsort(owner_order).astype(jnp.int32)
    quarter = N_PA // 4
    load = jnp.where(owner_rank < quarter, 2 * PD, jnp.where(owner_rank < 3 * quarter, PD, 0))
    begin = 2 * PD * jnp.minimum(owner_rank, quarter) + PD * jnp.clip(owner_rank - quarter, 0, 2 * quarter)
    shuffles = jax.vmap(lambda one_key: jax.random.permutation(one_key, CAP))(jax.random.split(slot_key, N_PA))
    listed = begin[:, None] + shuffles
    scorer = listed % N_PA
    within = listed // N_PA
    filled = jnp.where(shuffles < load[:, None], scorer * PD + within, -1)
    return filled.reshape(N_PA * CAP).astype(jnp.int32)


def draw_custodian_document_index(key, part):
    group_keys = jax.random.split(jax.random.fold_in(key, 11), N_PB)
    return jax.vmap(owner_group)(group_keys)


def touch_ends(values, key, least, top_value):
    extent = values.shape
    index_at = [jax.random.randint(jax.random.fold_in(key, axis), (), 0, extent[axis]) for axis in range(len(extent))]
    values = values.at[tuple(index_at)].set(least)
    longest = extent.index(max(extent))
    index_at[longest] = (index_at[longest] + 1) % extent[longest]
    return values.at[tuple(index_at)].set(top_value)


def level_of(stream_key, dims, shards, least, high):
    factor_of = 1.0
    for position, shards_of in shards:
        steps = jax.random.uniform(jax.random.fold_in(jax.random.fold_in(stream_key, 6), position), (shards_of,), jnp.float32, least / len(shards), high / len(shards))
        factor_of = factor_of * jnp.repeat(jnp.exp(steps), dims[position] // shards_of).reshape((-1,) + (1,) * (len(dims) - 1 - position))
    return factor_of


def gaussian(rng, shape, spread, most, cuts=(), kind=jnp.bfloat16):
    array = jax.random.normal(rng, shape, jnp.float32) * spread
    if len(cuts) > 0:
        array = level_of(rng, shape, cuts, -0.22, 0.18) * array
    return jnp.clip(array, min=-most, max=most).astype(kind)


def setup_inputs(seed: int = 0) -> dict:
    splits = jax.random.split(jax.random.key(seed), 7)
    return {
        "queries": draw_queries(jax.random.fold_in(splits[6], 71), 0),
        "encoder_outputs": gaussian(splits[1], (N_PB, N_PA * CAP, LEN, H), 1.0, 6.0, ((0, 16), (1, 16))),
        "proj_weight": gaussian(splits[2], (H, DIM), H ** -0.5, 0.1875),
        "bm25_rank": touch_ends(jax.random.randint(splits[3], (Q, N_PA, M), 0, 2 * DEPTH), jax.random.fold_in(splits[3], 1), 0, (2 * DEPTH) - 1).astype(jnp.int32),
        "dense_rank": touch_ends(jax.random.randint(splits[4], (Q, N_PA, M), 0, 2 * DEPTH), jax.random.fold_in(splits[4], 1), 0, (2 * DEPTH) - 1).astype(jnp.int32),
        "custodian_document_index": draw_custodian_document_index(jax.random.fold_in(splits[6], 71), 0),
    }


tau = 0.05
inv_temp = 20.0
rrf_offset = 60.0
norm_eps = 1e-06

def normalize(hid_rows, weight):
    projected = jnp.dot(hid_rows, weight, preferred_element_type=jnp.float32)
    scaling = lax.rsqrt(lax.optimization_barrier(jnp.sum(projected * projected, axis=-1, keepdims=True)) + norm_eps)
    return (projected * scaling, scaling)

def joined_target(bm25_rank, dense_rank):
    first = jnp.where(bm25_rank < DEPTH, rrf_offset / (rrf_offset + bm25_rank.astype(jnp.float32)), 0.0)
    second = jnp.where(dense_rank < DEPTH, rrf_offset / (rrf_offset + dense_rank.astype(jnp.float32)), 0.0)
    return (first + second).astype(jnp.float32)

def similarity(query_rows, key_block):
    flat_keys = key_block.reshape(PD * LEN, DIM)
    raw = jnp.dot(query_rows, flat_keys.T, preferred_element_type=jnp.float32) * inv_temp
    return raw.reshape(query_rows.shape[0], PD, LEN)

def log_total(raw):
    largest = lax.optimization_barrier(jnp.max(raw, axis=2, keepdims=True))
    return largest[:, :, 0] + jnp.log(lax.optimization_barrier(jnp.sum(jnp.exp(raw - largest), axis=2)))

def reference(queries, encoder_outputs, proj_weight, bm25_rank, dense_rank, custodian_document_index):
    holders = N_PA * PD
    blocks_all = N_PA * N_PB

    def embedding_cluster(packed):
        hid_group, slot_ids = packed
        unit_rows, scaling = normalize(hid_group.reshape(-1, H), proj_weight)
        emb_rows = unit_rows.astype(jnp.bfloat16).reshape(N_PA * CAP, LEN, DIM)
        target_at = jnp.where(slot_ids >= 0, slot_ids, holders).astype(jnp.int32)
        positioned_rows = jnp.zeros((holders, LEN, DIM), jnp.bfloat16).at[target_at].set(emb_rows, mode='drop')
        return (unit_rows, scaling, positioned_rows)
    task_portions, multiplier_list, positioned_rows = lax.map(embedding_cluster, (encoder_outputs, custodian_document_index))
    key_blocks = positioned_rows.reshape(N_PB, N_PA, PD, LEN, DIM).transpose(1, 0, 2, 3, 4)
    key_blocks = key_blocks.reshape(blocks_all, PD, LEN, DIM)
    lse_blocks = lax.map(lambda key_block: log_total(similarity(queries, key_block)), key_blocks)
    score = lse_blocks.reshape(blocks_all, Q, QT, PD).sum(axis=2) * (tau / QT)
    score = score.reshape(N_PA, N_PB, Q, PD).transpose(2, 0, 1, 3).reshape(Q, N_PA, M)
    residual = (score - joined_target(bm25_rank, dense_rank)).astype(jnp.bfloat16)
    residual_blocks = residual.astype(jnp.float32).reshape(Q, N_PA, N_PB, PD).transpose(1, 2, 0, 3)
    residual_blocks = residual_blocks.reshape(blocks_all, Q, PD)

    def backward_block(query_acc, packed):
        key_block, lse_block, residual_block = packed
        raw = similarity(queries, key_block)
        weights = jnp.exp(raw - lse_block[:, :, None])
        per_row = jnp.repeat(residual_block, QT, axis=0)
        coefficient = ((per_row / QT)[:, :, None] * weights).astype(jnp.bfloat16).reshape(Q * QT, PD * LEN)
        query_acc = query_acc + jnp.dot(coefficient, key_block.reshape(PD * LEN, DIM), preferred_element_type=jnp.float32)
        emb_part = jnp.dot(coefficient.T, queries, preferred_element_type=jnp.float32)
        return (query_acc, emb_part.astype(jnp.bfloat16))
    query_grad, emb_grad = lax.scan(backward_block, jnp.zeros((Q * QT, DIM), jnp.float32), (key_blocks, lse_blocks, residual_blocks))
    vector_groupings = emb_grad.reshape(N_PA, N_PB, PD, LEN, DIM).transpose(1, 0, 2, 3, 4).reshape(N_PB, holders, LEN, DIM)

    def custodian_reverse_traversal(packed):
        slot_ids, unit_rows, scaling, grads_group = packed
        filled = slot_ids >= 0
        picked = jnp.take(grads_group, jnp.clip(slot_ids, 0, holders - 1).astype(jnp.int32), axis=0)
        picked = jnp.where(filled[:, None, None], picked, jnp.zeros((), jnp.bfloat16))
        slot_grad = picked.astype(jnp.float32).reshape(-1, DIM)
        inner = lax.optimization_barrier(jnp.sum(unit_rows * slot_grad, axis=-1, keepdims=True))
        proj_grad = ((slot_grad - unit_rows * inner) * scaling).astype(jnp.bfloat16)
        hid_grad = jnp.dot(proj_grad, proj_weight.T, preferred_element_type=jnp.float32).astype(jnp.bfloat16)
        return hid_grad.reshape(N_PA * CAP, LEN, H)
    encoder_output_derivative = lax.map(custodian_reverse_traversal, (custodian_document_index, task_portions, multiplier_list, vector_groupings))
    return (query_grad, encoder_output_derivative)
```

```python
import math

import jax
import jax.numpy as jnp
from jax import lax
from jax.experimental import pallas as pl
from jax.experimental.pallas import tpu as pltpu
from jax.sharding import PartitionSpec as P

DIM = 128
H = 1024
QT = 32
LEN = 128
PD = 8
DEPTH = 100
CAP = 16
ROWS = CAP * LEN
GROUPS = 16
GR = 256
GQ = GR // QT

tau = 0.05
inv_temp = 20.0
rrf_offset = 60.0
norm_eps = 1e-06
log2_scale = inv_temp / math.log(2.0)

bf16 = jnp.bfloat16
f32 = jnp.float32
NT = (((1,), (1,)), ((), ()))
NN = (((1,), (0,)), ((), ()))
HIGH = lax.Precision.HIGHEST


def swap(value, axis, mask):
    return lax.ppermute(value, axis, [(i, i ^ mask) for i in range(16)])


def shift_x(value, by):
    return lax.ppermute(
        value, "pb", [(i, ((((i >> 2) + by) % 4) << 2) | (i & 3)) for i in range(16)]
    )


SHIFTS = (0, 1, -1, 2)


def gather_pb(value):
    pair = jnp.stack([value, swap(value, "pb", 2)])
    plane = jnp.stack([pair] + [shift_x(pair, by) for by in SHIFTS[1:]])
    return jnp.stack([plane, swap(plane, "pb", 1)])


def reduce_pb(parts):
    plane = (parts[0].astype(f32) + swap(parts[1], "pb", 1).astype(f32)).astype(bf16)
    got = [shift_x(plane[a], -SHIFTS[a]) for a in (1, 2, 3)]
    pair = plane[0].astype(f32)
    for one in got:
        pair = pair + one.astype(f32)
    return pair[0] + swap(pair[1].astype(bf16), "pb", 2).astype(f32)


def gather_pa(value):
    low = jnp.stack([value] + [swap(value, "pa", j) for j in (1, 2, 3)])
    return jnp.concatenate([low] + [swap(low, "pa", 4 * j) for j in (1, 2, 3)])


def reduce_pa(value, me):
    ids = jnp.arange(16, dtype=jnp.int32)
    order = (ids[None, :] == (ids[:, None] ^ me)).astype(bf16)
    blocks = lax.dot_general(
        order, value.astype(bf16).reshape(16, 16 * DIM), NN, preferred_element_type=f32
    ).astype(bf16)
    blocks = blocks.reshape(4, 4, 16, DIM)
    total = blocks[:, 0].astype(f32)
    for j in (1, 2, 3):
        total = total + swap(blocks[:, j], "pa", j).astype(f32)
    blocks = total.astype(bf16)
    total = total[0]
    for j in (1, 2, 3):
        total = total + swap(blocks[j], "pa", 4 * j).astype(f32)
    return total


def project_kernel(hid_ref, w_ref, proj_ref, emb_ref, emb_t_ref):
    proj = lax.dot_general(hid_ref[...], w_ref[...], NN, preferred_element_type=f32)
    scaling = lax.rsqrt(jnp.sum(proj * proj, axis=-1, keepdims=True) + norm_eps)
    unit = proj * scaling
    proj_ref[...] = proj
    emb_ref[...] = unit.astype(bf16)
    emb_t_ref[...] = unit.T.astype(bf16)


def project(hid, weight):
    step = 512
    return pl.pallas_call(
        project_kernel,
        grid=(ROWS // step,),
        in_specs=[
            pl.BlockSpec((step, H), lambda i: (i, 0)),
            pl.BlockSpec((H, DIM), lambda i: (0, 0)),
        ],
        out_specs=[
            pl.BlockSpec((step, DIM), lambda i: (i, 0)),
            pl.BlockSpec((step, DIM), lambda i: (i, 0)),
            pl.BlockSpec((DIM, step), lambda i: (0, i)),
        ],
        out_shape=[
            jax.ShapeDtypeStruct((ROWS, DIM), f32),
            jax.ShapeDtypeStruct((ROWS, DIM), bf16),
            jax.ShapeDtypeStruct((DIM, ROWS), bf16),
        ],
        compiler_params=pltpu.CompilerParams(vmem_limit_bytes=24 * 2**20),
        cost_estimate=pl.CostEstimate(
            flops=2 * ROWS * H * DIM, bytes_accessed=ROWS * (2 * H + 8 * DIM), transcendentals=0
        ),
        name="project",
    )(hid, weight)


def score_kernel(q_ref, emb_ref, emb_t_ref, pick_ref, target_ref, qg_ref, eg_ref, p_ref, c_ref):
    g = pl.program_id(0)

    @pl.when(g == 0)
    def _():
        eg_ref[...] = jnp.zeros_like(eg_ref)

    queries = q_ref[0, :GR, :]
    tops, sums = [], []
    for k in range(CAP):
        rows = slice(k * LEN, (k + 1) * LEN)
        raw = lax.dot_general(emb_ref[rows, :], queries, NT, preferred_element_type=f32)
        top = jnp.max(raw, axis=0, keepdims=True)
        p = jnp.exp2((raw - top) * log2_scale)
        p_ref[rows, :] = p
        tops.append(top)
        sums.append(jnp.sum(p, axis=0, keepdims=True))
    top = jnp.concatenate(tops, axis=0)
    total = jnp.concatenate(sums, axis=0)
    lse = inv_temp * top + jnp.log(total)
    row_q = lax.broadcasted_iota(jnp.int32, (GR, GR), 0) // QT
    col_q = lax.broadcasted_iota(jnp.int32, (GR, GR), 1) // QT
    same = (row_q == col_q).astype(f32)
    score = lax.dot_general(lse, same, NN, precision=HIGH, preferred_element_type=f32) * (tau / QT)
    wide = (
        lax.broadcasted_iota(jnp.int32, (LEN, GR), 0)
        == g * GQ + lax.broadcasted_iota(jnp.int32, (LEN, GR), 1) // QT
    ).astype(f32)
    pick = pick_ref[...]
    own = lax.dot_general(pick, target_ref[...], NN, precision=HIGH, preferred_element_type=f32)
    target = lax.dot_general(own, wide, NN, precision=HIGH, preferred_element_type=f32)
    residual = (score - target).astype(bf16).astype(f32) * jnp.sum(pick, axis=1, keepdims=True)
    factor = (residual / QT) / total
    for k in range(CAP):
        rows = slice(k * LEN, (k + 1) * LEN)
        c_ref[rows, :] = (p_ref[rows, :] * factor[k : k + 1, :]).astype(bf16)
    eg_ref[...] += lax.dot_general(c_ref[...], queries, NN, preferred_element_type=f32)
    qg = lax.dot_general(emb_t_ref[...], c_ref[...], NN, preferred_element_type=f32)
    qg_ref[0] = qg.T.astype(bf16)


def score_and_gradients(gathered, emb, emb_t, pick, target):
    height = gathered.shape[1]
    return pl.pallas_call(
        score_kernel,
        grid=(GROUPS,),
        in_specs=[
            pl.BlockSpec((1, height, DIM), lambda g: (g, 0, 0)),
            pl.BlockSpec((ROWS, DIM), lambda g: (0, 0)),
            pl.BlockSpec((DIM, ROWS), lambda g: (0, 0)),
            pl.BlockSpec((CAP, LEN), lambda g: (0, 0)),
            pl.BlockSpec((LEN, LEN), lambda g: (0, 0)),
        ],
        out_specs=[
            pl.BlockSpec((1, GR, DIM), lambda g: (g, 0, 0)),
            pl.BlockSpec((ROWS, DIM), lambda g: (0, 0)),
        ],
        out_shape=[
            jax.ShapeDtypeStruct((GROUPS, GR, DIM), bf16),
            jax.ShapeDtypeStruct((ROWS, DIM), f32),
        ],
        scratch_shapes=[pltpu.VMEM((ROWS, GR), f32), pltpu.VMEM((ROWS, GR), bf16)],
        compiler_params=pltpu.CompilerParams(vmem_limit_bytes=32 * 2**20),
        cost_estimate=pl.CostEstimate(
            flops=6 * GROUPS * GR * ROWS * DIM,
            bytes_accessed=5 * 2**20,
            transcendentals=GROUPS * GR * ROWS,
        ),
        name="score_and_gradients",
    )(gathered, emb, emb_t, pick, target)


def hidden_kernel(eg_ref, proj_ref, w_ref, out_ref):
    proj = proj_ref[...]
    scaling = lax.rsqrt(jnp.sum(proj * proj, axis=-1, keepdims=True) + norm_eps)
    unit = proj * scaling
    slot_grad = eg_ref[...].astype(bf16).astype(f32)
    inner = jnp.sum(unit * slot_grad, axis=-1, keepdims=True)
    proj_grad = ((slot_grad - unit * inner) * scaling).astype(bf16)
    out_ref[...] = lax.dot_general(
        proj_grad, w_ref[...], NT, preferred_element_type=f32
    ).astype(bf16)


def hidden_gradient(emb_grad, proj, weight):
    step = 512
    return pl.pallas_call(
        hidden_kernel,
        grid=(ROWS // step,),
        in_specs=[
            pl.BlockSpec((step, DIM), lambda i: (i, 0)),
            pl.BlockSpec((step, DIM), lambda i: (i, 0)),
            pl.BlockSpec((H, DIM), lambda i: (0, 0)),
        ],
        out_specs=pl.BlockSpec((step, H), lambda i: (i, 0)),
        out_shape=jax.ShapeDtypeStruct((ROWS, H), bf16),
        compiler_params=pltpu.CompilerParams(vmem_limit_bytes=24 * 2**20),
        cost_estimate=pl.CostEstimate(
            flops=2 * ROWS * H * DIM, bytes_accessed=ROWS * (2 * H + 8 * DIM), transcendentals=0
        ),
        name="hidden_gradient",
    )(emb_grad, proj, weight)


def rank_term(rank):
    return jnp.where(rank < DEPTH, rrf_offset / (rrf_offset + rank), 0.0)


def on_device(
    queries, encoder_outputs, proj_weight, bm25_rank, dense_rank, custodian_document_index
):
    me_pb, me_pa = lax.axis_index("pb"), lax.axis_index("pa")
    ids = jnp.arange(LEN, dtype=jnp.int32)
    slot_ids = custodian_document_index[0]
    place = jnp.where(slot_ids >= 0, slot_ids ^ (me_pa * PD), -1)
    pick = (place[:, None] == ids[None, :]).astype(f32)
    ranks = jnp.concatenate([bm25_rank[:, 0, :], dense_rank[:, 0, :]]).astype(bf16)
    gathered = gather_pb(jnp.concatenate([queries, ranks])).reshape(GROUPS, GR + 2 * GQ, DIM)
    proj, emb, emb_t = project(encoder_outputs.reshape(ROWS, H), proj_weight)
    own = (ids[None, :] == me_pb * PD + jnp.arange(PD, dtype=jnp.int32)[:, None]).astype(bf16)
    ranks = jnp.einsum("lm,grm->lgr", own, gathered[:, GR:, :], preferred_element_type=f32)
    target = rank_term(ranks[:, :, :GQ]) + rank_term(ranks[:, :, GQ:])
    target = gather_pa(target.reshape(PD, LEN)).reshape(LEN, LEN)
    query_parts, emb_grad = score_and_gradients(gathered, emb, emb_t, pick, target)
    own_sum = reduce_pb(query_parts.reshape(2, 4, 2, GR, DIM))
    query_grad = reduce_pa(own_sum, me_pa)
    hidden = hidden_gradient(emb_grad, proj, proj_weight)
    return (query_grad, hidden.reshape(1, CAP, LEN, H))


def solution(mesh):
    return jax.shard_map(
        on_device,
        mesh=mesh,
        in_specs=(
            P("pb", None),
            P("pb", "pa", None, None),
            P(),
            P("pb", "pa", None),
            P("pb", "pa", None),
            P("pb", "pa"),
        ),
        out_specs=(P(("pb", "pa"), None), P("pb", "pa", None, None)),
        check_vma=False,
    )
```

```python
import functools
import math

import jax
import jax.numpy as jnp
from jax import lax
from jax.experimental import pallas as pl
from jax.experimental.pallas import tpu as pltpu
from jax.sharding import PartitionSpec as P

DIM = 128
H = 1024
QT = 32
LEN = 128
PD = 8
DEPTH = 100
CAP = 16
ROWS = CAP * LEN
GROUPS = 16
GR = 256
GQ = GR // QT

tau = 0.05
inv_temp = 20.0
rrf_offset = 60.0
norm_eps = 1e-06
log2_scale = inv_temp / math.log(2.0)

bf16 = jnp.bfloat16
f32 = jnp.float32
NT = (((1,), (1,)), ((), ()))
NN = (((1,), (0,)), ((), ()))
HIGH = lax.Precision.HIGHEST


def swap(value, axis, mask):
    return lax.ppermute(value, axis, [(i, i ^ mask) for i in range(16)])


def shift_x(value, by):
    return lax.ppermute(
        value, "pb", [(i, ((((i >> 2) + by) % 4) << 2) | (i & 3)) for i in range(16)]
    )


SHIFTS = (0, 1, -1, 2)


def reduce_pa(value, me):
    ids = jnp.arange(16, dtype=jnp.int32)
    order = (ids[None, :] == (ids[:, None] ^ me)).astype(bf16)
    blocks = lax.dot_general(
        order, value.astype(bf16).reshape(16, 16 * DIM), NN, preferred_element_type=f32
    ).astype(bf16)
    blocks = blocks.reshape(4, 4, 16, DIM)
    total = blocks[:, 0].astype(f32)
    for j in (1, 2, 3):
        total = total + swap(blocks[:, j], "pa", j).astype(f32)
    blocks = total.astype(bf16)
    total = total[0]
    for j in (1, 2, 3):
        total = total + swap(blocks[j], "pa", 4 * j).astype(f32)
    return total


def project_kernel(hid_ref, w_ref, proj_ref, emb_ref, emb_t_ref):
    proj = lax.dot_general(hid_ref[...], w_ref[...], NN, preferred_element_type=f32)
    scaling = lax.rsqrt(jnp.sum(proj * proj, axis=-1, keepdims=True) + norm_eps)
    unit = proj * scaling
    proj_ref[...] = proj
    emb_ref[...] = unit.astype(bf16)
    emb_t_ref[...] = unit.T.astype(bf16)


def project(hid, weight):
    step = 512
    return pl.pallas_call(
        project_kernel,
        grid=(ROWS // step,),
        in_specs=[
            pl.BlockSpec((step, H), lambda i: (i, 0)),
            pl.BlockSpec((H, DIM), lambda i: (0, 0)),
        ],
        out_specs=[
            pl.BlockSpec((step, DIM), lambda i: (i, 0)),
            pl.BlockSpec((step, DIM), lambda i: (i, 0)),
            pl.BlockSpec((DIM, step), lambda i: (0, i)),
        ],
        out_shape=[
            jax.ShapeDtypeStruct((ROWS, DIM), f32),
            jax.ShapeDtypeStruct((ROWS, DIM), bf16),
            jax.ShapeDtypeStruct((DIM, ROWS), bf16),
        ],
        compiler_params=pltpu.CompilerParams(vmem_limit_bytes=6 * 2**20),
        cost_estimate=pl.CostEstimate(
            flops=2 * ROWS * H * DIM, bytes_accessed=ROWS * (2 * H + 8 * DIM), transcendentals=0
        ),
        name="project",
    )(hid, weight)


def token_sums(value):
    high = value.astype(bf16)
    rest = value - high.astype(f32)
    middle = rest.astype(bf16)
    low = (rest - middle.astype(f32)).astype(bf16)
    row_q = lax.broadcasted_iota(jnp.int32, (GR, GR), 0) // QT
    col_q = lax.broadcasted_iota(jnp.int32, (GR, GR), 1) // QT
    same = (row_q == col_q).astype(f32).astype(bf16)
    parts = [lax.dot_general(v, same, NN, preferred_element_type=f32) for v in (high, middle, low)]
    return parts[0] + (parts[1] + parts[2])


def forward_kernel(q_ref, emb_ref, p_ref, lse_ref, total_ref):
    queries = q_ref[0, :GR, :]
    tops, sums = [], []
    for k in range(CAP):
        rows = slice(k * LEN, (k + 1) * LEN)
        raw = lax.dot_general(emb_ref[rows, :], queries, NT, preferred_element_type=f32)
        top = jnp.max(raw, axis=0, keepdims=True)
        p = jnp.exp2((raw - top) * log2_scale)
        p_ref[0, rows, :] = p.astype(bf16)
        tops.append(top)
        sums.append(jnp.sum(p, axis=0, keepdims=True))
    top = jnp.concatenate(tops, axis=0)
    total = jnp.concatenate(sums, axis=0)
    lse_ref[0] = inv_temp * top + jnp.log(total)
    total_ref[0] = total


def forward(gathered, start, count, emb):
    height = gathered.shape[1]
    return pl.pallas_call(
        forward_kernel,
        grid=(count,),
        in_specs=[
            pl.BlockSpec((1, height, DIM), lambda g: (g + start, 0, 0)),
            pl.BlockSpec((ROWS, DIM), lambda g: (0, 0)),
        ],
        out_specs=[
            pl.BlockSpec((1, ROWS, GR), lambda g: (g, 0, 0)),
            pl.BlockSpec((1, CAP, GR), lambda g: (g, 0, 0)),
            pl.BlockSpec((1, CAP, GR), lambda g: (g, 0, 0)),
        ],
        out_shape=[
            jax.ShapeDtypeStruct((count, ROWS, GR), bf16),
            jax.ShapeDtypeStruct((count, CAP, GR), f32),
            jax.ShapeDtypeStruct((count, CAP, GR), f32),
        ],
        compiler_params=pltpu.CompilerParams(vmem_limit_bytes=6 * 2**20),
        cost_estimate=pl.CostEstimate(
            flops=2 * count * GR * ROWS * DIM,
            bytes_accessed=count * 2 * GR * ROWS,
            transcendentals=count * GR * ROWS,
        ),
        name="forward",
    )(gathered, emb)


def backward_kernel(
    first, half, q_at, q_ref, p_ref, lse_ref, total_ref, emb_t_ref, pick_ref, *rest
):
    target_refs = rest[:4]
    qg_ref, eg_ref, c_ref, own_ref, score_ref = rest[-5:]
    g = pl.program_id(0)
    pick = pick_ref[...]

    @pl.when(g == 0)
    def _():
        eg_ref[...] = jnp.zeros_like(eg_ref) if first else rest[4][...]
        own = jnp.zeros((CAP, LEN), f32)
        for j in range(4):
            part = target_refs[j][:, :, half * LEN : (half + 1) * LEN].reshape(QT, LEN)
            own += lax.dot_general(
                pick[:, j * QT : (j + 1) * QT], part, NN, precision=HIGH, preferred_element_type=f32
            )
        own_ref[...] = own
        score = token_sums(lse_ref[...].reshape(-1, GR)) * (tau / QT)
        score_ref[...] = score.reshape(score_ref.shape)

    queries = q_ref[0, :GR, :]
    held = jnp.sum(pick, axis=1, keepdims=True)
    own = own_ref[...]
    lane = lax.broadcasted_iota(jnp.int32, (CAP, LEN), 1) // QT
    factors = []
    for k in range(2):
        lanes = slice(k * LEN, (k + 1) * LEN)
        at = lane + ((g + q_at) * 2 * GQ + k * (GQ // 2))
        target = jnp.take_along_axis(own, at, axis=1, mode="promise_in_bounds")
        residual = (score_ref[g, :, lanes] - target).astype(bf16).astype(f32) * held
        factors.append((residual / QT) / total_ref[0, :, lanes])
    factor = jnp.concatenate(factors, axis=1)
    for k in range(CAP):
        rows = slice(k * LEN, (k + 1) * LEN)
        c_ref[rows, :] = (p_ref[0, rows, :].astype(f32) * factor[k : k + 1, :]).astype(bf16)
    eg_ref[...] += lax.dot_general(c_ref[...], queries, NN, preferred_element_type=f32)
    qg = lax.dot_general(emb_t_ref[...], c_ref[...], NN, preferred_element_type=f32)
    qg_ref[0] = qg.T.astype(bf16)


def backward(gathered, start, half, kept, emb_t, pick, targets, emb_grad=None):
    height = gathered.shape[1]
    p, lse, total = kept
    count = p.shape[0]
    first = emb_grad is None
    whole = lambda g: (0, 0)
    step = lambda g: (g, 0, 0)
    in_specs = [
        pl.BlockSpec((1, height, DIM), lambda g: (g + start, 0, 0)),
        pl.BlockSpec((1, ROWS, GR), step),
        pl.BlockSpec((count, CAP, GR), lambda g: (0, 0, 0)),
        pl.BlockSpec((1, CAP, GR), step),
        pl.BlockSpec((DIM, ROWS), whole),
        pl.BlockSpec((CAP, LEN), whole),
    ] + [pl.BlockSpec((4, PD, 2 * LEN), lambda g: (0, 0, 0))] * 4
    args = [gathered, p, lse, total, emb_t, pick, *targets]
    if not first:
        in_specs.append(pl.BlockSpec((ROWS, DIM), whole))
        args.append(emb_grad)
    return pl.pallas_call(
        functools.partial(backward_kernel, first, half, start),
        grid=(count,),
        in_specs=in_specs,
        out_specs=[pl.BlockSpec((1, GR, DIM), step), pl.BlockSpec((ROWS, DIM), whole)],
        out_shape=[
            jax.ShapeDtypeStruct((count, GR, DIM), bf16),
            jax.ShapeDtypeStruct((ROWS, DIM), f32),
        ],
        scratch_shapes=[pltpu.VMEM((ROWS, GR), bf16), pltpu.VMEM((CAP, LEN), f32), pltpu.VMEM((count, CAP, GR), f32)],
        compiler_params=pltpu.CompilerParams(vmem_limit_bytes=11 * 2**20),
        cost_estimate=pl.CostEstimate(
            flops=4 * count * GR * ROWS * DIM,
            bytes_accessed=count * 2 * GR * ROWS,
            transcendentals=0,
        ),
        name="backward",
    )(*args)


def hidden_kernel(eg_ref, proj_ref, w_ref, out_ref):
    proj = proj_ref[...]
    scaling = lax.rsqrt(jnp.sum(proj * proj, axis=-1, keepdims=True) + norm_eps)
    unit = proj * scaling
    slot_grad = eg_ref[...].astype(bf16).astype(f32)
    inner = jnp.sum(unit * slot_grad, axis=-1, keepdims=True)
    proj_grad = ((slot_grad - unit * inner) * scaling).astype(bf16)
    out_ref[...] = lax.dot_general(
        proj_grad, w_ref[...], NT, preferred_element_type=f32
    ).astype(bf16)


def hidden_gradient(emb_grad, proj, weight):
    step = 512
    return pl.pallas_call(
        hidden_kernel,
        grid=(ROWS // step,),
        in_specs=[
            pl.BlockSpec((step, DIM), lambda i: (i, 0)),
            pl.BlockSpec((step, DIM), lambda i: (i, 0)),
            pl.BlockSpec((H, DIM), lambda i: (0, 0)),
        ],
        out_specs=pl.BlockSpec((step, H), lambda i: (i, 0)),
        out_shape=jax.ShapeDtypeStruct((ROWS, H), bf16),
        compiler_params=pltpu.CompilerParams(vmem_limit_bytes=8 * 2**20),
        cost_estimate=pl.CostEstimate(
            flops=2 * ROWS * H * DIM, bytes_accessed=ROWS * (2 * H + 8 * DIM), transcendentals=0
        ),
        name="hidden_gradient",
    )(emb_grad, proj, weight)


def target_kernel(me_ref, near_ref, far_ref, out_ref):
    row = lax.broadcasted_iota(jnp.int32, (2 * PD, LEN), 0) + me_ref[0] * PD
    own = (row == lax.broadcasted_iota(jnp.int32, (2 * PD, LEN), 1)).astype(f32).astype(bf16)
    for half, ref in enumerate((near_ref, far_ref)):
        ranks = ref[...].reshape(LEN, LEN)
        rank = lax.dot_general(own, ranks, NT, preferred_element_type=f32)[:PD]
        term = rank_term(rank)
        out_ref[:, half * LEN : (half + 1) * LEN] = term + pltpu.roll(term, LEN - GQ, 1)


def targets_of(me_pb, near, far):
    rows = pl.BlockSpec((8, 2 * GQ, DIM), lambda i: (0, GR // (2 * GQ), 0))
    return pl.pallas_call(
        target_kernel,
        grid=(1,),
        in_specs=[pl.BlockSpec(memory_space=pltpu.SMEM), rows, rows],
        out_specs=pl.BlockSpec((PD, 2 * LEN), lambda i: (0, 0)),
        out_shape=jax.ShapeDtypeStruct((PD, 2 * LEN), f32),
        compiler_params=pltpu.CompilerParams(vmem_limit_bytes=2 * 2**20),
        name="targets",
    )(me_pb.reshape(1), near, far)


def rank_term(rank):
    return jnp.where(rank < DEPTH, rrf_offset / (rrf_offset + rank), 0.0)


def on_device(
    queries, encoder_outputs, proj_weight, bm25_rank, dense_rank, custodian_document_index
):
    me_pb, me_pa = lax.axis_index("pb"), lax.axis_index("pa")
    ids = jnp.arange(LEN, dtype=jnp.int32)
    slot_ids = custodian_document_index[0]
    place = jnp.where(slot_ids >= 0, slot_ids ^ (me_pa * PD), -1)
    pick = (place[:, None] == ids[None, :]).astype(f32)
    ranks = jnp.concatenate([bm25_rank[:, 0, :], dense_rank[:, 0, :]]).astype(bf16)
    mine = jnp.concatenate([queries, ranks])
    other = swap(mine, "pb", 2)
    proj, emb, emb_t = project(encoder_outputs.reshape(ROWS, H), proj_weight)
    pair = jnp.stack([mine, other])
    got = [shift_x(pair, by) for by in SHIFTS[1:]]
    kept_d = forward(pair, 0, 2, emb)
    got, kept_d = lax.optimization_barrier((got, kept_d))
    plane = jnp.concatenate([pair] + got)
    far = swap(plane, "pb", 1)
    kept_b = forward(plane, 2, 6, emb)
    far, kept_b = lax.optimization_barrier((far, kept_b))
    target = targets_of(me_pb, plane, far)
    low = [swap(target, "pa", j) for j in (1, 2, 3)]
    kept_a = forward(far, 2, 6, emb)
    low, kept_a = lax.optimization_barrier((low, kept_a))
    low = jnp.stack([target] + low)
    high = [swap(low, "pa", 4 * j) for j in (1, 2, 3)]
    kept_c = forward(far, 0, 2, emb)
    high, kept_c = lax.optimization_barrier((high, kept_c))
    own_args = (emb_t, pick, [low] + high)
    qg_a, eg = backward(far, 2, 1, kept_a, *own_args)
    from_core = swap(qg_a, "pb", 1)
    qg_b, eg = backward(plane, 2, 0, kept_b, *own_args, eg)
    sent = (qg_b.astype(f32) + from_core.astype(f32)).astype(bf16).reshape(3, 2, GR, DIM)
    from_x = [shift_x(sent[a - 1], -SHIFTS[a]) for a in (1, 2, 3)]
    qg_c, eg = backward(far, 0, 1, kept_c, *own_args, eg)
    from_core = swap(qg_c, "pb", 1)
    qg_d, eg = backward(pair, 0, 0, kept_d, *own_args, eg)
    hidden = hidden_gradient(eg, proj, proj_weight)
    from_x, hidden = lax.optimization_barrier((from_x, hidden))
    both = qg_d.astype(f32) + from_core.astype(f32)
    for one in from_x:
        both = both + one.astype(f32)
    from_y = swap(both[1].astype(bf16), "pb", 2)
    query_grad = reduce_pa(both[0] + from_y.astype(f32), me_pa)
    return (query_grad, hidden.reshape(1, CAP, LEN, H))


def solution(mesh):
    return jax.shard_map(
        on_device,
        mesh=mesh,
        in_specs=(
            P("pb", None),
            P("pb", "pa", None, None),
            P(),
            P("pb", "pa", None),
            P("pb", "pa", None),
            P("pb", "pa"),
        ),
        out_specs=(P(("pb", "pa"), None), P("pb", "pa", None, None)),
        check_vma=False,
    )
```

```python
import functools
import math

import jax
import jax.numpy as jnp
from jax import lax
from jax.experimental import pallas as pl
from jax.experimental.pallas import tpu as pltpu
from jax.sharding import PartitionSpec as P

DIM = 128
H = 1024
QT = 32
LEN = 128
PD = 8
DEPTH = 100
CAP = 16
ROWS = CAP * LEN
GROUPS = 16
GR = 256
GQ = GR // QT

tau = 0.05
inv_temp = 20.0
rrf_offset = 60.0
norm_eps = 1e-06
log2_scale = inv_temp / math.log(2.0)

bf16 = jnp.bfloat16
f32 = jnp.float32
NT = (((1,), (1,)), ((), ()))
NN = (((1,), (0,)), ((), ()))
HIGH = lax.Precision.HIGHEST


def swap(value, axis, mask):
    return lax.ppermute(value, axis, [(i, i ^ mask) for i in range(16)])


def shift_x(value, by):
    return lax.ppermute(
        value, "pb", [(i, ((((i >> 2) + by) % 4) << 2) | (i & 3)) for i in range(16)]
    )


SHIFTS = (0, 1, -1, 2)


def shift_z(value, by):
    return lax.ppermute(
        value, "pa", [(i, ((((i >> 1) + by) % 8) << 1) | (i & 1)) for i in range(16)]
    )


Z_PLACE = (0, 2, 7, 6, 4, 3, 5, 1)
Z_OFFSETS = (0, 1, 7, 3, 4, 2, 5, 6)


def swap_y(value, low, high):
    pairs = [(i, i ^ (32 * low + high)) for i in range(256)]
    return lax.ppermute(value, ("pb", "pa"), pairs)


def order_of(me):
    j = jnp.arange(16, dtype=jnp.int32)[:, None]
    offset = jnp.zeros_like(j)
    for place, one in enumerate(Z_OFFSETS):
        offset = jnp.where((j & 7) == place, one, offset)
    block = ((((me >> 1) + offset) & 7) << 1) + ((me & 1) ^ (j >> 3))
    return (block == jnp.arange(16, dtype=jnp.int32)[None, :]).astype(bf16)


def reduce_y_z(value, order):
    blocks = [
        lax.dot_general(
            order, rows.astype(bf16).reshape(16, 16 * DIM), NN, preferred_element_type=f32
        )
        .astype(bf16)
        .reshape(2, 8, 16, DIM)
        for rows in value
    ]
    got = [swap_y(blocks[1][1], 1, 1), swap_y(blocks[0][1], 0, 1), swap_y(blocks[1][0], 1, 0)]
    blocks = blocks[0][0].astype(f32)
    for one in got:
        blocks = blocks + one.astype(f32)
    up = shift_z(blocks[3:6].astype(bf16), 3).astype(f32)
    down = shift_z(blocks[6:].astype(bf16), -3).astype(f32)
    near_up = (blocks[1] + up[1] + down[1]).astype(bf16)
    near_down = (blocks[2] + up[2]).astype(bf16)
    up_one, down_one = shift_z(near_up, 1), shift_z(near_down, -1)
    return blocks[0] + up[0] + down[0] + up_one.astype(f32) + down_one.astype(f32)


def project_kernel(hid_ref, w_ref, proj_ref, emb_ref, emb_t_ref):
    proj = lax.dot_general(hid_ref[...], w_ref[...], NN, preferred_element_type=f32)
    scaling = lax.rsqrt(jnp.sum(proj * proj, axis=-1, keepdims=True) + norm_eps)
    unit = proj * scaling
    proj_ref[...] = proj
    emb_ref[...] = unit.astype(bf16)
    emb_t_ref[...] = unit.T.astype(bf16)


def project(hid, weight):
    step = 512
    return pl.pallas_call(
        project_kernel,
        grid=(ROWS // step,),
        in_specs=[
            pl.BlockSpec((step, H), lambda i: (i, 0)),
            pl.BlockSpec((H, DIM), lambda i: (0, 0)),
        ],
        out_specs=[
            pl.BlockSpec((step, DIM), lambda i: (i, 0)),
            pl.BlockSpec((step, DIM), lambda i: (i, 0)),
            pl.BlockSpec((DIM, step), lambda i: (0, i)),
        ],
        out_shape=[
            jax.ShapeDtypeStruct((ROWS, DIM), f32),
            jax.ShapeDtypeStruct((ROWS, DIM), bf16),
            jax.ShapeDtypeStruct((DIM, ROWS), bf16),
        ],
        compiler_params=pltpu.CompilerParams(vmem_limit_bytes=6 * 2**20),
        cost_estimate=pl.CostEstimate(
            flops=2 * ROWS * H * DIM, bytes_accessed=ROWS * (2 * H + 8 * DIM), transcendentals=0
        ),
        name="project",
    )(*(pltpu.with_memory_space_constraint(x, pltpu.HBM) for x in (hid, weight)))


def token_sums(value):
    high = value.astype(bf16)
    rest = value - high.astype(f32)
    middle = rest.astype(bf16)
    low = (rest - middle.astype(f32)).astype(bf16)
    row_q = lax.broadcasted_iota(jnp.int32, (GR, GR), 0) // QT
    col_q = lax.broadcasted_iota(jnp.int32, (GR, GR), 1) // QT
    same = (row_q == col_q).astype(f32).astype(bf16)
    parts = [lax.dot_general(v, same, NN, preferred_element_type=f32) for v in (high, middle, low)]
    return parts[0] + (parts[1] + parts[2])


def forward_kernel(q_ref, emb_ref, p_ref, lse_ref, total_ref):
    queries = q_ref[0, :GR, :]
    tops, sums = [], []
    for k in range(CAP):
        rows = slice(k * LEN, (k + 1) * LEN)
        raw = lax.dot_general(emb_ref[rows, :], queries, NT, preferred_element_type=f32)
        top = jnp.max(raw, axis=0, keepdims=True)
        p = jnp.exp2((raw - top) * log2_scale)
        p_ref[0, rows, :] = p.astype(bf16)
        tops.append(top)
        sums.append(jnp.sum(p, axis=0, keepdims=True))
    top = jnp.concatenate(tops, axis=0)
    total = jnp.concatenate(sums, axis=0)
    lse_ref[0] = inv_temp * top + jnp.log(total)
    total_ref[0] = total


def forward(gathered, start, count, emb):
    height = gathered.shape[1]
    return pl.pallas_call(
        forward_kernel,
        grid=(count,),
        in_specs=[
            pl.BlockSpec((1, height, DIM), lambda g: (g + start, 0, 0)),
            pl.BlockSpec((ROWS, DIM), lambda g: (0, 0)),
        ],
        out_specs=[
            pl.BlockSpec((1, ROWS, GR), lambda g: (g, 0, 0)),
            pl.BlockSpec((1, CAP, GR), lambda g: (g, 0, 0)),
            pl.BlockSpec((1, CAP, GR), lambda g: (g, 0, 0)),
        ],
        out_shape=[
            jax.ShapeDtypeStruct((count, ROWS, GR), bf16),
            jax.ShapeDtypeStruct((count, CAP, GR), f32),
            jax.ShapeDtypeStruct((count, CAP, GR), f32),
        ],
        compiler_params=pltpu.CompilerParams(vmem_limit_bytes=6 * 2**20),
        cost_estimate=pl.CostEstimate(
            flops=2 * count * GR * ROWS * DIM,
            bytes_accessed=count * 2 * GR * ROWS,
            transcendentals=count * GR * ROWS,
        ),
        name="forward",
    )(gathered, emb)


def backward_kernel(
    first, half, q_at, q_ref, p_ref, lse_ref, total_ref, emb_t_ref, pick_ref, *rest
):
    target_refs = rest[:3]
    qg_ref, eg_ref, c_ref, own_ref, score_ref = rest[-5:]
    g = pl.program_id(0)

    @pl.when(g == 0)
    def _():
        eg_ref[...] = jnp.zeros_like(eg_ref) if first else rest[3][...]
        own = jnp.zeros((CAP, LEN), f32)
        for j in range(3):
            part = target_refs[j][:, :, half * LEN : (half + 1) * LEN].reshape(6 * PD, LEN)
            own += lax.dot_general(
                pick_ref[j], part, NN, precision=HIGH, preferred_element_type=f32
            )
        own_ref[...] = own
        score = token_sums(lse_ref[...].reshape(-1, GR)) * (tau / QT)
        score_ref[...] = score.reshape(score_ref.shape)

    queries = q_ref[:, :GR, :].reshape(2 * GR, DIM)
    pick = pick_ref[...]
    held = jnp.sum(pick[0] + pick[1] + pick[2], axis=1, keepdims=True)
    own = own_ref[...]
    lane = lax.broadcasted_iota(jnp.int32, (CAP, LEN), 1) // QT
    for u in range(2):
        factors = []
        for k in range(2):
            lanes = slice(k * LEN, (k + 1) * LEN)
            at = lane + ((2 * g + u + q_at) * 2 * GQ + k * (GQ // 2))
            target = jnp.take_along_axis(own, at, axis=1, mode="promise_in_bounds")
            residual = (score_ref[2 * g + u, :, lanes] - target).astype(bf16).astype(f32) * held
            factors.append((residual / QT) / total_ref[u, :, lanes])
        factor = jnp.concatenate(factors, axis=1)
        for k in range(CAP):
            rows = slice(k * LEN, (k + 1) * LEN)
            c_ref[rows, u * GR : (u + 1) * GR] = (
                p_ref[u, rows, :].astype(f32) * factor[k : k + 1, :]
            ).astype(bf16)
    eg_ref[...] += lax.dot_general(c_ref[...], queries, NN, preferred_element_type=f32)
    qg = lax.dot_general(emb_t_ref[...], c_ref[...], NN, preferred_element_type=f32)
    qg_ref[...] = qg.T.astype(bf16).reshape(2, GR, DIM)


def backward(gathered, start, half, kept, emb_t, pick, targets, emb_grad=None):
    height = gathered.shape[1]
    p, lse, total = kept
    count = p.shape[0]
    first = emb_grad is None
    whole = lambda g: (0, 0)
    step = lambda g: (g, 0, 0)
    fixed = lambda g: (0, 0, 0)
    in_specs = [
        pl.BlockSpec((2, height, DIM), lambda g: (g + start // 2, 0, 0)),
        pl.BlockSpec((2, ROWS, GR), step),
        pl.BlockSpec((count, CAP, GR), fixed),
        pl.BlockSpec((2, CAP, GR), step),
        pl.BlockSpec((DIM, ROWS), whole),
        pl.BlockSpec((3, CAP, 6 * PD), fixed),
    ] + [pl.BlockSpec((6, PD, 2 * LEN), fixed)] * 3
    args = [gathered, p, lse, total, emb_t, pick, *targets]
    if not first:
        in_specs.append(pl.BlockSpec((ROWS, DIM), whole))
        args.append(emb_grad)
    return pl.pallas_call(
        functools.partial(backward_kernel, first, half, start),
        grid=(count // 2,),
        in_specs=in_specs,
        out_specs=[pl.BlockSpec((2, GR, DIM), step), pl.BlockSpec((ROWS, DIM), whole)],
        out_shape=[
            jax.ShapeDtypeStruct((count, GR, DIM), bf16),
            jax.ShapeDtypeStruct((ROWS, DIM), f32),
        ],
        scratch_shapes=[
            pltpu.VMEM((ROWS, 2 * GR), bf16),
            pltpu.VMEM((CAP, LEN), f32),
            pltpu.VMEM((count, CAP, GR), f32),
        ],
        compiler_params=pltpu.CompilerParams(vmem_limit_bytes=14 * 2**20),
        cost_estimate=pl.CostEstimate(
            flops=4 * count * GR * ROWS * DIM,
            bytes_accessed=count * 2 * GR * ROWS,
            transcendentals=0,
        ),
        name="backward",
    )(*args)


def hidden_kernel(eg_ref, proj_ref, w_ref, out_ref):
    proj = proj_ref[...]
    scaling = lax.rsqrt(jnp.sum(proj * proj, axis=-1, keepdims=True) + norm_eps)
    unit = proj * scaling
    slot_grad = eg_ref[...].astype(bf16).astype(f32)
    inner = jnp.sum(unit * slot_grad, axis=-1, keepdims=True)
    proj_grad = ((slot_grad - unit * inner) * scaling).astype(bf16)
    out_ref[...] = lax.dot_general(
        proj_grad, w_ref[...], NT, preferred_element_type=f32
    ).astype(bf16)


def hidden_gradient(emb_grad, proj, weight):
    step = 512
    return pl.pallas_call(
        hidden_kernel,
        grid=(ROWS // step,),
        in_specs=[
            pl.BlockSpec((step, DIM), lambda i: (i, 0)),
            pl.BlockSpec((step, DIM), lambda i: (i, 0)),
            pl.BlockSpec((H, DIM), lambda i: (0, 0)),
        ],
        out_specs=pl.BlockSpec((step, H), lambda i: (i, 0)),
        out_shape=jax.ShapeDtypeStruct((ROWS, H), bf16),
        compiler_params=pltpu.CompilerParams(vmem_limit_bytes=8 * 2**20),
        cost_estimate=pl.CostEstimate(
            flops=2 * ROWS * H * DIM, bytes_accessed=ROWS * (2 * H + 8 * DIM), transcendentals=0
        ),
        name="hidden_gradient",
    )(emb_grad, proj, weight)


def target_kernel(first_ref, near_ref, far_ref, out_ref):
    row = lax.broadcasted_iota(jnp.int32, (2 * PD, LEN), 0) + first_ref[0]
    own = (row == lax.broadcasted_iota(jnp.int32, (2 * PD, LEN), 1)).astype(f32).astype(bf16)
    for half, ref in enumerate((near_ref, far_ref)):
        ranks = ref[...].reshape(LEN, LEN)
        rank = lax.dot_general(own, ranks, NT, preferred_element_type=f32)[:PD]
        term = rank_term(rank)
        out_ref[:, half * LEN : (half + 1) * LEN] = term + pltpu.roll(term, LEN - GQ, 1)


def targets_of(first_row, near, far):
    rows = pl.BlockSpec((8, 2 * GQ, DIM), lambda i: (0, GR // (2 * GQ), 0))
    return pl.pallas_call(
        target_kernel,
        grid=(1,),
        in_specs=[pl.BlockSpec(memory_space=pltpu.SMEM), rows, rows],
        out_specs=pl.BlockSpec((PD, 2 * LEN), lambda i: (0, 0)),
        out_shape=jax.ShapeDtypeStruct((PD, 2 * LEN), f32),
        compiler_params=pltpu.CompilerParams(vmem_limit_bytes=2 * 2**20),
        name="targets",
    )(first_row, near, far)


def rank_term(rank):
    return jnp.where(rank < DEPTH, rrf_offset / (rrf_offset + rank), 0.0)


def on_device(
    queries, encoder_outputs, proj_weight, bm25_rank, dense_rank, custodian_document_index
):
    me_pb, me_pa = lax.axis_index("pb"), lax.axis_index("pa")
    slot_ids = custodian_document_index[0]
    shard = slot_ids >> 3
    offset = ((shard >> 1) - (me_pa >> 1)) & 7
    place = jnp.zeros_like(offset)
    for at, one in enumerate(Z_PLACE):
        place = jnp.where(offset == at, one, place)
    place = (place * 2 + ((shard ^ me_pa) & 1)) * PD + (slot_ids & 7)
    place = jnp.where(slot_ids >= 0, place, -1)
    rows = jnp.arange(18 * PD, dtype=jnp.int32).reshape(3, 1, 6 * PD)
    pick = (place[None, :, None] == rows).astype(f32)
    ranks = jnp.concatenate([bm25_rank[:, 0, :], dense_rank[:, 0, :]]).astype(bf16)
    mine = jnp.concatenate([queries, ranks])
    other = swap(mine, "pb", 2)
    first_row, order = (me_pb * PD).reshape(1), order_of(me_pa)
    other, late_weight, pick, order, first_row = lax.optimization_barrier(
        (other, proj_weight, pick, order, first_row)
    )
    proj, emb, emb_t = project(encoder_outputs.reshape(ROWS, H), late_weight)
    pair = jnp.stack([mine, other])
    got = [shift_x(pair, by) for by in SHIFTS[1:]]
    kept_d = forward(pair, 0, 2, emb)
    got, kept_d = lax.optimization_barrier((got, kept_d))
    plane = jnp.concatenate([pair] + got)
    far = swap(plane, "pb", 1)
    kept_b = forward(plane, 2, 6, emb)
    far, kept_b = lax.optimization_barrier((far, kept_b))
    target = targets_of(first_row, plane, far)
    from_y = swap(target, "pa", 1)
    kept_c = forward(far, 0, 2, emb)
    from_y, kept_c = lax.optimization_barrier((from_y, kept_c))
    targets = jnp.stack([target, from_y])
    from_z = [shift_z(targets, 1), shift_z(targets, -1)]
    kept_a = forward(far, 2, 2, emb)
    from_z, kept_a = lax.optimization_barrier((from_z, kept_a))
    targets = jnp.concatenate([targets] + from_z)
    from_z = [shift_z(targets, 3), shift_z(targets, -3)]
    kept_e = forward(far, 4, 4, emb)
    from_z, kept_e = lax.optimization_barrier((from_z, kept_e))
    own_args = (emb_t, pick, [targets] + from_z)
    qg_e, eg = backward(far, 4, 1, kept_e, *own_args)
    from_core = [swap(qg_e, "pb", 1)]
    qg_a, eg = backward(far, 2, 1, kept_a, *own_args, eg)
    from_core = jnp.concatenate([swap(qg_a, "pb", 1)] + from_core)
    qg_b, eg = backward(plane, 2, 0, kept_b, *own_args, eg)
    sent = (qg_b.astype(f32) + from_core.astype(f32)).astype(bf16).reshape(3, 2, GR, DIM)
    from_x = [shift_x(sent[a - 1], -SHIFTS[a]) for a in (1, 2, 3)]
    qg_c, eg = backward(far, 0, 1, kept_c, *own_args, eg)
    from_core = swap(qg_c, "pb", 1)
    qg_d, eg = backward(pair, 0, 0, kept_d, *own_args, eg)
    hidden = hidden_gradient(eg, proj, proj_weight)
    from_x, hidden = lax.optimization_barrier((from_x, hidden))
    both = qg_d.astype(f32) + from_core.astype(f32)
    for one in from_x:
        both = both + one.astype(f32)
    query_grad = reduce_y_z(both, order)
    return (query_grad, hidden.reshape(1, CAP, LEN, H))


def solution(mesh):
    return jax.shard_map(
        on_device,
        mesh=mesh,
        in_specs=(
            P("pb", None),
            P("pb", "pa", None, None),
            P(),
            P("pb", "pa", None),
            P("pb", "pa", None),
            P("pb", "pa"),
        ),
        out_specs=(P(("pb", "pa"), None), P("pb", "pa", None, None)),
        check_vma=False,
    )
```

```python
import functools
import math

import jax
import jax.numpy as jnp
from jax import lax
from jax.experimental import pallas as pl
from jax.experimental.pallas import tpu as pltpu
from jax.sharding import PartitionSpec as P

DIM = 128
H = 1024
QT = 32
LEN = 128
PD = 8
DEPTH = 100
CAP = 16
ROWS = CAP * LEN
GROUPS = 16
GR = 256
GQ = GR // QT

tau = 0.05
inv_temp = 20.0
rrf_offset = 60.0
norm_eps = 1e-06
log2_scale = inv_temp / math.log(2.0)

bf16 = jnp.bfloat16
f32 = jnp.float32
NT = (((1,), (1,)), ((), ()))
NN = (((1,), (0,)), ((), ()))
HIGH = lax.Precision.HIGHEST


def swap(value, axis, mask):
    return lax.ppermute(value, axis, [(i, i ^ mask) for i in range(16)])


def shift_x(value, by):
    return lax.ppermute(
        value, "pb", [(i, ((((i >> 2) + by) % 4) << 2) | (i & 3)) for i in range(16)]
    )


SHIFTS = (0, 1, -1, 2)


def shift_z(value, by):
    return lax.ppermute(
        value, "pa", [(i, ((((i >> 1) + by) % 8) << 1) | (i & 1)) for i in range(16)]
    )


Z_PLACE = (0, 2, 7, 6, 4, 3, 5, 1)
Z_OFFSETS = (0, 1, 7, 3, 4, 2, 5, 6)


def swap_y(value, low, high):
    pairs = [(i, i ^ (32 * low + high)) for i in range(256)]
    return lax.ppermute(value, ("pb", "pa"), pairs)


def order_of(me):
    j = jnp.arange(16, dtype=jnp.int32)[:, None]
    offset = jnp.zeros_like(j)
    for place, one in enumerate(Z_OFFSETS):
        offset = jnp.where((j & 7) == place, one, offset)
    block = ((((me >> 1) + offset) & 7) << 1) + ((me & 1) ^ (j >> 3))
    return (block == jnp.arange(16, dtype=jnp.int32)[None, :]).astype(bf16)


def reduce_y_z(value, order):
    blocks = [
        lax.dot_general(
            order, rows.astype(bf16).reshape(16, 16 * DIM), NN, preferred_element_type=f32
        )
        .astype(bf16)
        .reshape(2, 8, 16, DIM)
        for rows in value
    ]
    got = [swap_y(blocks[1][1], 1, 1), swap_y(blocks[0][1], 0, 1), swap_y(blocks[1][0], 1, 0)]
    blocks = blocks[0][0].astype(f32)
    for one in got:
        blocks = blocks + one.astype(f32)
    up = shift_z(blocks[3:6].astype(bf16), 3).astype(f32)
    down = shift_z(blocks[6:].astype(bf16), -3).astype(f32)
    near_up = (blocks[1] + up[1] + down[1]).astype(bf16)
    near_down = (blocks[2] + up[2]).astype(bf16)
    up_one, down_one = shift_z(near_up, 1), shift_z(near_down, -1)
    return blocks[0] + up[0] + down[0] + up_one.astype(f32) + down_one.astype(f32)


def project_kernel(hid_ref, w_ref, proj_ref, emb_ref, emb_t_ref):
    proj = lax.dot_general(hid_ref[...], w_ref[...], NN, preferred_element_type=f32)
    scaling = lax.rsqrt(jnp.sum(proj * proj, axis=-1, keepdims=True) + norm_eps)
    unit = proj * scaling
    proj_ref[...] = proj
    emb_ref[...] = unit.astype(bf16)
    emb_t_ref[...] = unit.T.astype(bf16)


def project(hid, weight):
    step = 1024
    return pl.pallas_call(
        project_kernel,
        grid=(ROWS // step,),
        in_specs=[
            pl.BlockSpec((step, H), lambda i: (i, 0)),
            pl.BlockSpec((H, DIM), lambda i: (0, 0)),
        ],
        out_specs=[
            pl.BlockSpec((step, DIM), lambda i: (i, 0)),
            pl.BlockSpec((step, DIM), lambda i: (i, 0)),
            pl.BlockSpec((DIM, step), lambda i: (0, i)),
        ],
        out_shape=[
            jax.ShapeDtypeStruct((ROWS, DIM), f32),
            jax.ShapeDtypeStruct((ROWS, DIM), bf16),
            jax.ShapeDtypeStruct((DIM, ROWS), bf16),
        ],
        compiler_params=pltpu.CompilerParams(vmem_limit_bytes=12 * 2**20),
        cost_estimate=pl.CostEstimate(
            flops=2 * ROWS * H * DIM, bytes_accessed=ROWS * (2 * H + 8 * DIM), transcendentals=0
        ),
        name="project",
    )(*(pltpu.with_memory_space_constraint(x, pltpu.HBM) for x in (hid, weight)))


def token_sums(value):
    high = value.astype(bf16)
    rest = value - high.astype(f32)
    middle = rest.astype(bf16)
    low = (rest - middle.astype(f32)).astype(bf16)
    row_q = lax.broadcasted_iota(jnp.int32, (GR, GR), 0) // QT
    col_q = lax.broadcasted_iota(jnp.int32, (GR, GR), 1) // QT
    same = (row_q == col_q).astype(f32).astype(bf16)
    parts = [lax.dot_general(v, same, NN, preferred_element_type=f32) for v in (high, middle, low)]
    return parts[0] + (parts[1] + parts[2])


def forward_kernel(q_ref, emb_ref, *rest):
    p_ref, lse_ref, total_ref = rest[-3:]
    queries = q_ref[0, :GR, :]
    tops, sums = [], []
    for k in range(CAP):
        rows = slice(k * LEN, (k + 1) * LEN)
        raw = lax.dot_general(emb_ref[rows, :], queries, NT, preferred_element_type=f32)
        top = jnp.max(raw, axis=0, keepdims=True)
        p = jnp.exp2((raw - top) * log2_scale)
        p_ref[0, rows, :] = p.astype(bf16)
        tops.append(top)
        sums.append(jnp.sum(p, axis=0, keepdims=True))
    top = jnp.concatenate(tops, axis=0)
    total = jnp.concatenate(sums, axis=0)
    lse_ref[0] = inv_temp * top + jnp.log(total)
    total_ref[0] = total


def forward(gathered, start, count, emb, place, size, kept=(), after=()):
    height = gathered.shape[1]
    step = lambda g: (g + place, 0, 0)
    return pl.pallas_call(
        forward_kernel,
        grid=(count,),
        in_specs=[
            pl.BlockSpec((1, height, DIM), lambda g: (g + start, 0, 0)),
            pl.BlockSpec((ROWS, DIM), lambda g: (0, 0)),
        ]
        + [pl.BlockSpec(memory_space=pl.ANY)] * (len(kept) + len(after)),
        out_specs=[
            pl.BlockSpec((1, ROWS, GR), step),
            pl.BlockSpec((1, CAP, GR), step),
            pl.BlockSpec((1, CAP, GR), step),
        ],
        out_shape=[
            jax.ShapeDtypeStruct((size, ROWS, GR), bf16),
            jax.ShapeDtypeStruct((size, CAP, GR), f32),
            jax.ShapeDtypeStruct((size, CAP, GR), f32),
        ],
        input_output_aliases={2 + i: i for i in range(len(kept))},
        compiler_params=pltpu.CompilerParams(vmem_limit_bytes=6 * 2**20),
        cost_estimate=pl.CostEstimate(
            flops=2 * count * GR * ROWS * DIM // 4,
            bytes_accessed=count * 2 * GR * ROWS // 4,
            transcendentals=count * GR * ROWS // 4,
        ),
        name="forward",
    )(gathered, emb, *kept, *after)


def backward_kernel(
    first, half, q_at, q_ref, p_ref, lse_ref, total_ref, emb_t_ref, pick_ref, *rest
):
    target_refs = rest[:3]
    qg_ref, eg_ref, c_ref, own_ref, score_ref = rest[-5:]
    g = pl.program_id(0)

    @pl.when(g == 0)
    def _():
        eg_ref[...] = jnp.zeros_like(eg_ref) if first else rest[3][...]
        own = jnp.zeros((CAP, LEN), f32)
        for j in range(3):
            part = target_refs[j][:, :, half * LEN : (half + 1) * LEN].reshape(6 * PD, LEN)
            own += lax.dot_general(
                pick_ref[j], part, NN, precision=HIGH, preferred_element_type=f32
            )
        own_ref[...] = own
        score = token_sums(lse_ref[...].reshape(-1, GR)) * (tau / QT)
        score_ref[...] = score.reshape(score_ref.shape)

    queries = q_ref[:, :GR, :].reshape(2 * GR, DIM)
    pick = pick_ref[...]
    held = jnp.sum(pick[0] + pick[1] + pick[2], axis=1, keepdims=True)
    own = own_ref[...]
    lane = lax.broadcasted_iota(jnp.int32, (CAP, LEN), 1) // QT
    for u in range(2):
        factors = []
        for k in range(2):
            lanes = slice(k * LEN, (k + 1) * LEN)
            at = lane + ((2 * g + u + q_at) * 2 * GQ + k * (GQ // 2))
            target = jnp.take_along_axis(own, at, axis=1, mode="promise_in_bounds")
            residual = (score_ref[2 * g + u, :, lanes] - target).astype(bf16).astype(f32) * held
            factors.append((residual / QT) / total_ref[u, :, lanes])
        factor = jnp.concatenate(factors, axis=1)
        for k in range(CAP):
            rows = slice(k * LEN, (k + 1) * LEN)
            c_ref[rows, u * GR : (u + 1) * GR] = (
                p_ref[u, rows, :].astype(f32) * factor[k : k + 1, :]
            ).astype(bf16)
    eg_ref[...] += lax.dot_general(c_ref[...], queries, NN, preferred_element_type=f32)
    qg = lax.dot_general(emb_t_ref[...], c_ref[...], NN, preferred_element_type=f32)
    qg_ref[...] = qg.T.astype(bf16).reshape(2, GR, DIM)


def backward(gathered, start, half, kept, emb_t, pick, targets, emb_grad=None):
    height = gathered.shape[1]
    p, lse, total = kept
    count = p.shape[0]
    first = emb_grad is None
    whole = lambda g: (0, 0)
    step = lambda g: (g, 0, 0)
    fixed = lambda g: (0, 0, 0)
    in_specs = [
        pl.BlockSpec((2, height, DIM), lambda g: (g + start // 2, 0, 0)),
        pl.BlockSpec((2, ROWS, GR), step),
        pl.BlockSpec((count, CAP, GR), fixed),
        pl.BlockSpec((2, CAP, GR), step),
        pl.BlockSpec((DIM, ROWS), whole),
        pl.BlockSpec((3, CAP, 6 * PD), fixed),
    ] + [pl.BlockSpec((6, PD, 2 * LEN), fixed)] * 3
    args = [gathered, p, lse, total, emb_t, pick, *targets]
    if not first:
        in_specs.append(pl.BlockSpec((ROWS, DIM), whole))
        args.append(emb_grad)
    return pl.pallas_call(
        functools.partial(backward_kernel, first, half, start),
        grid=(count // 2,),
        in_specs=in_specs,
        out_specs=[pl.BlockSpec((2, GR, DIM), step), pl.BlockSpec((ROWS, DIM), whole)],
        out_shape=[
            jax.ShapeDtypeStruct((count, GR, DIM), bf16),
            jax.ShapeDtypeStruct((ROWS, DIM), f32),
        ],
        scratch_shapes=[
            pltpu.VMEM((ROWS, 2 * GR), bf16),
            pltpu.VMEM((CAP, LEN), f32),
            pltpu.VMEM((count, CAP, GR), f32),
        ],
        compiler_params=pltpu.CompilerParams(vmem_limit_bytes=14 * 2**20),
        cost_estimate=pl.CostEstimate(
            flops=4 * count * GR * ROWS * DIM,
            bytes_accessed=count * 2 * GR * ROWS,
            transcendentals=0,
        ),
        name="backward",
    )(*args)


def hidden_kernel(eg_ref, proj_ref, w_ref, out_ref):
    proj = proj_ref[...]
    scaling = lax.rsqrt(jnp.sum(proj * proj, axis=-1, keepdims=True) + norm_eps)
    unit = proj * scaling
    slot_grad = eg_ref[...].astype(bf16).astype(f32)
    inner = jnp.sum(unit * slot_grad, axis=-1, keepdims=True)
    proj_grad = ((slot_grad - unit * inner) * scaling).astype(bf16)
    out_ref[...] = lax.dot_general(
        proj_grad, w_ref[...], NT, preferred_element_type=f32
    ).astype(bf16)


def hidden_gradient(emb_grad, proj, weight):
    step = 1024
    return pl.pallas_call(
        hidden_kernel,
        grid=(ROWS // step,),
        in_specs=[
            pl.BlockSpec((step, DIM), lambda i: (i, 0)),
            pl.BlockSpec((step, DIM), lambda i: (i, 0)),
            pl.BlockSpec((H, DIM), lambda i: (0, 0)),
        ],
        out_specs=pl.BlockSpec((step, H), lambda i: (i, 0)),
        out_shape=jax.ShapeDtypeStruct((ROWS, H), bf16),
        compiler_params=pltpu.CompilerParams(vmem_limit_bytes=12 * 2**20),
        cost_estimate=pl.CostEstimate(
            flops=2 * ROWS * H * DIM, bytes_accessed=ROWS * (2 * H + 8 * DIM), transcendentals=0
        ),
        name="hidden_gradient",
    )(emb_grad, proj, weight)


def target_kernel(first_ref, near_ref, far_ref, out_ref):
    row = lax.broadcasted_iota(jnp.int32, (2 * PD, LEN), 0) + first_ref[0]
    own = (row == lax.broadcasted_iota(jnp.int32, (2 * PD, LEN), 1)).astype(f32).astype(bf16)
    for half, ref in enumerate((near_ref, far_ref)):
        ranks = ref[...].reshape(LEN, LEN)
        rank = lax.dot_general(own, ranks, NT, preferred_element_type=f32)[:PD]
        term = rank_term(rank)
        out_ref[:, half * LEN : (half + 1) * LEN] = term + pltpu.roll(term, LEN - GQ, 1)


def targets_of(first_row, near, far):
    rows = pl.BlockSpec((8, 2 * GQ, DIM), lambda i: (0, GR // (2 * GQ), 0))
    return pl.pallas_call(
        target_kernel,
        grid=(1,),
        in_specs=[pl.BlockSpec(memory_space=pltpu.SMEM), rows, rows],
        out_specs=pl.BlockSpec((PD, 2 * LEN), lambda i: (0, 0)),
        out_shape=jax.ShapeDtypeStruct((PD, 2 * LEN), f32),
        compiler_params=pltpu.CompilerParams(vmem_limit_bytes=2 * 2**20),
        name="targets",
    )(first_row, near, far)


def rank_term(rank):
    return jnp.where(rank < DEPTH, rrf_offset / (rrf_offset + rank), 0.0)


def on_device(
    queries, encoder_outputs, proj_weight, bm25_rank, dense_rank, custodian_document_index
):
    me_pb, me_pa = lax.axis_index("pb"), lax.axis_index("pa")
    slot_ids = custodian_document_index[0]
    shard = slot_ids >> 3
    offset = ((shard >> 1) - (me_pa >> 1)) & 7
    place = jnp.zeros_like(offset)
    for at, one in enumerate(Z_PLACE):
        place = jnp.where(offset == at, one, place)
    place = (place * 2 + ((shard ^ me_pa) & 1)) * PD + (slot_ids & 7)
    place = jnp.where(slot_ids >= 0, place, -1)
    rows = jnp.arange(18 * PD, dtype=jnp.int32).reshape(3, 1, 6 * PD)
    pick = (place[None, :, None] == rows).astype(f32)
    ranks = jnp.concatenate([bm25_rank[:, 0, :], dense_rank[:, 0, :]]).astype(bf16)
    mine = jnp.concatenate([queries, ranks])
    other = swap(mine, "pb", 2)
    first_row, order = (me_pb * PD).reshape(1), order_of(me_pa)
    other, late_weight, pick, order, first_row = lax.optimization_barrier(
        (other, proj_weight, pick, order, first_row)
    )
    proj, emb, emb_t = project(encoder_outputs.reshape(ROWS, H), late_weight)
    pair = jnp.stack([mine, other])
    got = [shift_x(pair, by) for by in SHIFTS[1:]]
    kept_d = forward(pair, 0, 2, emb, 0, 2)
    got, kept_d = lax.optimization_barrier((got, kept_d))
    plane = jnp.concatenate([pair] + got)
    far = swap(plane, "pb", 1)
    kept_b = forward(plane, 2, 4, emb, 0, 6)
    far, kept_b = lax.optimization_barrier((far, kept_b))
    target = targets_of(first_row, plane, far)
    from_y = swap(target, "pa", 1)
    kept_b = forward(plane, 6, 2, emb, 4, 6, kept_b, [target])
    kept_f = forward(far, 0, 2, emb, 0, 8, after=[target])
    from_y, kept_b, kept_f = lax.optimization_barrier((from_y, kept_b, kept_f))
    targets = jnp.stack([target, from_y])
    from_z = [shift_z(targets, 1), shift_z(targets, -1)]
    kept_f = forward(far, 2, 2, emb, 2, 8, kept_f)
    from_z, kept_f = lax.optimization_barrier((from_z, kept_f))
    targets = jnp.concatenate([targets] + from_z)
    from_z = [shift_z(targets, 3), shift_z(targets, -3)]
    kept_f = forward(far, 4, 4, emb, 4, 8, kept_f)
    from_z, kept_f = lax.optimization_barrier((from_z, kept_f))
    own_args = (emb_t, pick, [targets] + from_z)
    qg_f, eg = backward(far, 0, 1, kept_f, *own_args)
    from_core = swap(qg_f, "pb", 1)
    qg_b, eg = backward(plane, 2, 0, kept_b, *own_args, eg)
    sent = (qg_b.astype(f32) + from_core[2:].astype(f32)).astype(bf16).reshape(3, 2, GR, DIM)
    from_x = [shift_x(sent[a - 1], -SHIFTS[a]) for a in (1, 2, 3)]
    qg_d, eg = backward(pair, 0, 0, kept_d, *own_args, eg)
    hidden = hidden_gradient(eg, proj, proj_weight)
    from_x, hidden = lax.optimization_barrier((from_x, hidden))
    both = qg_d.astype(f32) + from_core[:2].astype(f32)
    for one in from_x:
        both = both + one.astype(f32)
    query_grad = reduce_y_z(both, order)
    return (query_grad, hidden.reshape(1, CAP, LEN, H))


def solution(mesh):
    return jax.shard_map(
        on_device,
        mesh=mesh,
        in_specs=(
            P("pb", None),
            P("pb", "pa", None, None),
            P(),
            P("pb", "pa", None),
            P("pb", "pa", None),
            P("pb", "pa"),
        ),
        out_specs=(P(("pb", "pa"), None), P("pb", "pa", None, None)),
        check_vma=False,
    )
```

```python
import functools
import math

import jax
import jax.numpy as jnp
from jax import lax
from jax.experimental import pallas as pl
from jax.experimental.pallas import tpu as pltpu
from jax.sharding import PartitionSpec as P

DIM = 128
H = 1024
QT = 32
LEN = 128
PD = 8
DEPTH = 100
CAP = 16
ROWS = CAP * LEN
GROUPS = 16
GR = 256
GQ = GR // QT

tau = 0.05
inv_temp = 20.0
rrf_offset = 60.0
norm_eps = 1e-06
log2_scale = inv_temp / math.log(2.0)

bf16 = jnp.bfloat16
f32 = jnp.float32
NT = (((1,), (1,)), ((), ()))
NN = (((1,), (0,)), ((), ()))
HIGH = lax.Precision.HIGHEST


def swap(value, axis, mask):
    return lax.ppermute(value, axis, [(i, i ^ mask) for i in range(16)])


def shift_x(value, by):
    return lax.ppermute(
        value, "pb", [(i, ((((i >> 2) + by) % 4) << 2) | (i & 3)) for i in range(16)]
    )


SHIFTS = (0, 1, -1, 2)


def shift_z(value, by):
    return lax.ppermute(
        value, "pa", [(i, ((((i >> 1) + by) % 8) << 1) | (i & 1)) for i in range(16)]
    )


Z_PLACE = (0, 2, 7, 6, 4, 3, 5, 1)
Z_OFFSETS = (0, 1, 7, 3, 4, 2, 5, 6)


def swap_y(value, low, high):
    pairs = [(i, i ^ (32 * low + high)) for i in range(256)]
    return lax.ppermute(value, ("pb", "pa"), pairs)


def order_of(me):
    j = jnp.arange(16, dtype=jnp.int32)[:, None]
    offset = jnp.zeros_like(j)
    for place, one in enumerate(Z_OFFSETS):
        offset = jnp.where((j & 7) == place, one, offset)
    block = ((((me >> 1) + offset) & 7) << 1) + ((me & 1) ^ (j >> 3))
    return (block == jnp.arange(16, dtype=jnp.int32)[None, :]).astype(bf16)


def reduce_y_z(value, order):
    blocks = [
        lax.dot_general(
            order, rows.astype(bf16).reshape(16, 16 * DIM), NN, preferred_element_type=f32
        )
        .astype(bf16)
        .reshape(2, 8, 16, DIM)
        for rows in value
    ]
    got = [swap_y(blocks[1][1], 1, 1), swap_y(blocks[0][1], 0, 1), swap_y(blocks[1][0], 1, 0)]
    blocks = blocks[0][0].astype(f32)
    for one in got:
        blocks = blocks + one.astype(f32)
    up = shift_z(blocks[3:6].astype(bf16), 3).astype(f32)
    down = shift_z(blocks[6:].astype(bf16), -3).astype(f32)
    near_up = (blocks[1] + up[1] + down[1]).astype(bf16)
    near_down = (blocks[2] + up[2]).astype(bf16)
    up_one, down_one = shift_z(near_up, 1), shift_z(near_down, -1)
    return blocks[0] + up[0] + down[0] + up_one.astype(f32) + down_one.astype(f32)


def join_kernel(query_ref, first_ref, second_ref, out_ref):
    out_ref[:GR, :] = query_ref[...]
    ranks = jnp.concatenate([first_ref[...], second_ref[...]])
    out_ref[GR:, :] = ranks.astype(f32).astype(bf16)


def join(queries, bm25_rank, dense_rank):
    return pl.pallas_call(
        join_kernel,
        out_shape=jax.ShapeDtypeStruct((GR + 2 * GQ, DIM), bf16),
        compiler_params=pltpu.CompilerParams(vmem_limit_bytes=2 * 2**20),
        name="join",
    )(
        *(
            pltpu.with_memory_space_constraint(x, pltpu.HBM)
            for x in (queries, bm25_rank, dense_rank)
        )
    )


def project_kernel(hid_ref, w_ref, proj_ref, emb_ref, emb_t_ref):
    proj = lax.dot_general(hid_ref[...], w_ref[...], NN, preferred_element_type=f32)
    scaling = lax.rsqrt(jnp.sum(proj * proj, axis=-1, keepdims=True) + norm_eps)
    unit = proj * scaling
    proj_ref[...] = proj
    emb_ref[...] = unit.astype(bf16)
    emb_t_ref[...] = unit.T.astype(bf16)


def project(hid, weight):
    step = 1024
    return pl.pallas_call(
        project_kernel,
        grid=(ROWS // step,),
        in_specs=[
            pl.BlockSpec((step, H), lambda i: (i, 0)),
            pl.BlockSpec((H, DIM), lambda i: (0, 0)),
        ],
        out_specs=[
            pl.BlockSpec((step, DIM), lambda i: (i, 0)),
            pl.BlockSpec((step, DIM), lambda i: (i, 0)),
            pl.BlockSpec((DIM, step), lambda i: (0, i)),
        ],
        out_shape=[
            jax.ShapeDtypeStruct((ROWS, DIM), f32),
            jax.ShapeDtypeStruct((ROWS, DIM), bf16),
            jax.ShapeDtypeStruct((DIM, ROWS), bf16),
        ],
        compiler_params=pltpu.CompilerParams(vmem_limit_bytes=12 * 2**20),
        cost_estimate=pl.CostEstimate(
            flops=2 * ROWS * H * DIM, bytes_accessed=ROWS * (2 * H + 8 * DIM), transcendentals=0
        ),
        name="project",
    )(*(pltpu.with_memory_space_constraint(x, pltpu.HBM) for x in (hid, weight)))


def token_sums(value):
    high = value.astype(bf16)
    rest = value - high.astype(f32)
    middle = rest.astype(bf16)
    low = (rest - middle.astype(f32)).astype(bf16)
    row_q = lax.broadcasted_iota(jnp.int32, (GR, GR), 0) // QT
    col_q = lax.broadcasted_iota(jnp.int32, (GR, GR), 1) // QT
    same = (row_q == col_q).astype(f32).astype(bf16)
    parts = [lax.dot_general(v, same, NN, preferred_element_type=f32) for v in (high, middle, low)]
    return parts[0] + (parts[1] + parts[2])


def forward_kernel(q_ref, emb_ref, *rest):
    p_ref, lse_ref, total_ref = rest[-3:]
    queries = q_ref[0, :GR, :]
    tops, sums = [], []
    for k in range(CAP):
        rows = slice(k * LEN, (k + 1) * LEN)
        raw = lax.dot_general(emb_ref[rows, :], queries, NT, preferred_element_type=f32)
        top = jnp.max(raw, axis=0, keepdims=True)
        p = jnp.exp2((raw - top) * log2_scale)
        p_ref[0, rows, :] = p.astype(bf16)
        tops.append(top)
        sums.append(jnp.sum(p, axis=0, keepdims=True))
    top = jnp.concatenate(tops, axis=0)
    total = jnp.concatenate(sums, axis=0)
    lse_ref[0] = inv_temp * top + jnp.log(total)
    total_ref[0] = total


def forward(gathered, start, count, emb, place, size, kept=(), after=()):
    height = gathered.shape[1]
    step = lambda g: (g + place, 0, 0)
    return pl.pallas_call(
        forward_kernel,
        grid=(count,),
        in_specs=[
            pl.BlockSpec((1, height, DIM), lambda g: (g + start, 0, 0)),
            pl.BlockSpec((ROWS, DIM), lambda g: (0, 0)),
        ]
        + [pl.BlockSpec(memory_space=pl.ANY)] * (len(kept) + len(after)),
        out_specs=[
            pl.BlockSpec((1, ROWS, GR), step),
            pl.BlockSpec((1, CAP, GR), step),
            pl.BlockSpec((1, CAP, GR), step),
        ],
        out_shape=[
            jax.ShapeDtypeStruct((size, ROWS, GR), bf16),
            jax.ShapeDtypeStruct((size, CAP, GR), f32),
            jax.ShapeDtypeStruct((size, CAP, GR), f32),
        ],
        input_output_aliases={2 + i: i for i in range(len(kept))},
        compiler_params=pltpu.CompilerParams(vmem_limit_bytes=6 * 2**20),
        cost_estimate=pl.CostEstimate(
            flops=2 * count * GR * ROWS * DIM // 4,
            bytes_accessed=count * 2 * GR * ROWS // 4,
            transcendentals=count * GR * ROWS // 4,
        ),
        name="forward",
    )(gathered, emb, *kept, *after)


def backward_kernel(
    first, half, q_at, q_ref, p_ref, lse_ref, total_ref, emb_t_ref, pick_ref, *rest
):
    target_refs = rest[:3]
    qg_ref, eg_ref, c_ref, own_ref, score_ref = rest[-5:]
    g = pl.program_id(0)

    @pl.when(g == 0)
    def _():
        eg_ref[...] = jnp.zeros_like(eg_ref) if first else rest[3][...]
        own = jnp.zeros((CAP, LEN), f32)
        for j in range(3):
            part = target_refs[j][:, :, half * LEN : (half + 1) * LEN].reshape(6 * PD, LEN)
            own += lax.dot_general(
                pick_ref[j], part, NN, precision=HIGH, preferred_element_type=f32
            )
        own_ref[...] = own
        score = token_sums(lse_ref[...].reshape(-1, GR)) * (tau / QT)
        score_ref[...] = score.reshape(score_ref.shape)

    queries = q_ref[:, :GR, :].reshape(2 * GR, DIM)
    pick = pick_ref[...]
    held = jnp.sum(pick[0] + pick[1] + pick[2], axis=1, keepdims=True)
    own = own_ref[...]
    lane = lax.broadcasted_iota(jnp.int32, (CAP, LEN), 1) // QT
    for u in range(2):
        factors = []
        for k in range(2):
            lanes = slice(k * LEN, (k + 1) * LEN)
            at = lane + ((2 * g + u + q_at) * 2 * GQ + k * (GQ // 2))
            target = jnp.take_along_axis(own, at, axis=1, mode="promise_in_bounds")
            residual = (score_ref[2 * g + u, :, lanes] - target).astype(bf16).astype(f32) * held
            factors.append((residual / QT) / total_ref[u, :, lanes])
        factor = jnp.concatenate(factors, axis=1)
        for k in range(CAP):
            rows = slice(k * LEN, (k + 1) * LEN)
            c_ref[rows, u * GR : (u + 1) * GR] = (
                p_ref[u, rows, :].astype(f32) * factor[k : k + 1, :]
            ).astype(bf16)
    eg_ref[...] += lax.dot_general(c_ref[...], queries, NN, preferred_element_type=f32)
    qg = lax.dot_general(emb_t_ref[...], c_ref[...], NN, preferred_element_type=f32)
    qg_ref[...] = qg.T.astype(bf16).reshape(2, GR, DIM)


def backward(gathered, start, half, kept, emb_t, pick, targets, emb_grad=None):
    height = gathered.shape[1]
    p, lse, total = kept
    count = p.shape[0]
    first = emb_grad is None
    whole = lambda g: (0, 0)
    step = lambda g: (g, 0, 0)
    fixed = lambda g: (0, 0, 0)
    in_specs = [
        pl.BlockSpec((2, height, DIM), lambda g: (g + start // 2, 0, 0)),
        pl.BlockSpec((2, ROWS, GR), step),
        pl.BlockSpec((count, CAP, GR), fixed),
        pl.BlockSpec((2, CAP, GR), step),
        pl.BlockSpec((DIM, ROWS), whole),
        pl.BlockSpec((3, CAP, 6 * PD), fixed),
    ] + [pl.BlockSpec((6, PD, 2 * LEN), fixed)] * 3
    args = [gathered, p, lse, total, emb_t, pick, *targets]
    if not first:
        in_specs.append(pl.BlockSpec((ROWS, DIM), whole))
        args.append(emb_grad)
    return pl.pallas_call(
        functools.partial(backward_kernel, first, half, start),
        grid=(count // 2,),
        in_specs=in_specs,
        out_specs=[pl.BlockSpec((2, GR, DIM), step), pl.BlockSpec((ROWS, DIM), whole)],
        out_shape=[
            jax.ShapeDtypeStruct((count, GR, DIM), bf16),
            jax.ShapeDtypeStruct((ROWS, DIM), f32),
        ],
        scratch_shapes=[
            pltpu.VMEM((ROWS, 2 * GR), bf16),
            pltpu.VMEM((CAP, LEN), f32),
            pltpu.VMEM((count, CAP, GR), f32),
        ],
        compiler_params=pltpu.CompilerParams(vmem_limit_bytes=14 * 2**20),
        cost_estimate=pl.CostEstimate(
            flops=4 * count * GR * ROWS * DIM,
            bytes_accessed=count * 2 * GR * ROWS,
            transcendentals=0,
        ),
        name="backward",
    )(*args)


def hidden_kernel(eg_ref, proj_ref, w_ref, out_ref):
    proj = proj_ref[...]
    scaling = lax.rsqrt(jnp.sum(proj * proj, axis=-1, keepdims=True) + norm_eps)
    unit = proj * scaling
    slot_grad = eg_ref[...].astype(bf16).astype(f32)
    inner = jnp.sum(unit * slot_grad, axis=-1, keepdims=True)
    proj_grad = ((slot_grad - unit * inner) * scaling).astype(bf16)
    out_ref[...] = lax.dot_general(
        proj_grad, w_ref[...], NT, preferred_element_type=f32
    ).astype(bf16)


def hidden_gradient(emb_grad, proj, weight):
    step = 1024
    return pl.pallas_call(
        hidden_kernel,
        grid=(ROWS // step,),
        in_specs=[
            pl.BlockSpec((step, DIM), lambda i: (i, 0)),
            pl.BlockSpec((step, DIM), lambda i: (i, 0)),
            pl.BlockSpec((H, DIM), lambda i: (0, 0)),
        ],
        out_specs=pl.BlockSpec((step, H), lambda i: (i, 0)),
        out_shape=jax.ShapeDtypeStruct((ROWS, H), bf16),
        compiler_params=pltpu.CompilerParams(vmem_limit_bytes=12 * 2**20),
        cost_estimate=pl.CostEstimate(
            flops=2 * ROWS * H * DIM, bytes_accessed=ROWS * (2 * H + 8 * DIM), transcendentals=0
        ),
        name="hidden_gradient",
    )(emb_grad, proj, weight)


def target_kernel(first_ref, near_ref, far_ref, out_ref):
    row = lax.broadcasted_iota(jnp.int32, (2 * PD, LEN), 0) + first_ref[0]
    own = (row == lax.broadcasted_iota(jnp.int32, (2 * PD, LEN), 1)).astype(f32).astype(bf16)
    for half, ref in enumerate((near_ref, far_ref)):
        ranks = ref[...].reshape(LEN, LEN)
        rank = lax.dot_general(own, ranks, NT, preferred_element_type=f32)[:PD]
        term = rank_term(rank)
        out_ref[:, half * LEN : (half + 1) * LEN] = term + pltpu.roll(term, LEN - GQ, 1)


def targets_of(first_row, near, far):
    rows = pl.BlockSpec((8, 2 * GQ, DIM), lambda i: (0, GR // (2 * GQ), 0))
    return pl.pallas_call(
        target_kernel,
        grid=(1,),
        in_specs=[pl.BlockSpec(memory_space=pltpu.SMEM), rows, rows],
        out_specs=pl.BlockSpec((PD, 2 * LEN), lambda i: (0, 0)),
        out_shape=jax.ShapeDtypeStruct((PD, 2 * LEN), f32),
        compiler_params=pltpu.CompilerParams(vmem_limit_bytes=2 * 2**20),
        name="targets",
    )(first_row, near, far)


def rank_term(rank):
    return jnp.where(rank < DEPTH, rrf_offset / (rrf_offset + rank), 0.0)


def on_device(
    queries, encoder_outputs, proj_weight, bm25_rank, dense_rank, custodian_document_index
):
    me_pb, me_pa = lax.axis_index("pb"), lax.axis_index("pa")
    slot_ids = custodian_document_index[0]
    shard = slot_ids >> 3
    offset = ((shard >> 1) - (me_pa >> 1)) & 7
    place = jnp.zeros_like(offset)
    for at, one in enumerate(Z_PLACE):
        place = jnp.where(offset == at, one, place)
    place = (place * 2 + ((shard ^ me_pa) & 1)) * PD + (slot_ids & 7)
    place = jnp.where(slot_ids >= 0, place, -1)
    rows = jnp.arange(18 * PD, dtype=jnp.int32).reshape(3, 1, 6 * PD)
    pick = (place[None, :, None] == rows).astype(f32)
    mine = join(queries, bm25_rank[:, 0, :], dense_rank[:, 0, :])
    other = swap(mine, "pb", 2)
    first_row, order = (me_pb * PD).reshape(1), order_of(me_pa)
    other, late_weight, pick, order, first_row = lax.optimization_barrier(
        (other, proj_weight, pick, order, first_row)
    )
    proj, emb, emb_t = project(encoder_outputs.reshape(ROWS, H), late_weight)
    pair = jnp.stack([mine, other])
    got = [shift_x(pair, by) for by in SHIFTS[1:]]
    kept_d = forward(pair, 0, 2, emb, 0, 2)
    got, kept_d = lax.optimization_barrier((got, kept_d))
    plane = jnp.concatenate([pair] + got)
    far = swap(plane, "pb", 1)
    kept_b = forward(plane, 2, 4, emb, 0, 6)
    far, kept_b = lax.optimization_barrier((far, kept_b))
    target = targets_of(first_row, plane, far)
    from_y = swap(target, "pa", 1)
    kept_b = forward(plane, 6, 2, emb, 4, 6, kept_b, [target])
    kept_f = forward(far, 0, 2, emb, 0, 8, after=[target])
    from_y, kept_b, kept_f = lax.optimization_barrier((from_y, kept_b, kept_f))
    targets = jnp.stack([target, from_y])
    from_z = [shift_z(targets, 1), shift_z(targets, -1)]
    kept_f = forward(far, 2, 2, emb, 2, 8, kept_f)
    from_z, kept_f = lax.optimization_barrier((from_z, kept_f))
    targets = jnp.concatenate([targets] + from_z)
    from_z = [shift_z(targets, 3), shift_z(targets, -3)]
    kept_f = forward(far, 4, 4, emb, 4, 8, kept_f)
    from_z, kept_f = lax.optimization_barrier((from_z, kept_f))
    own_args = (emb_t, pick, [targets] + from_z)
    qg_f, eg = backward(far, 0, 1, kept_f, *own_args)
    from_core = swap(qg_f, "pb", 1)
    qg_b, eg = backward(plane, 2, 0, kept_b, *own_args, eg)
    sent = (qg_b.astype(f32) + from_core[2:].astype(f32)).astype(bf16).reshape(3, 2, GR, DIM)
    from_x = [shift_x(sent[a - 1], -SHIFTS[a]) for a in (1, 2, 3)]
    qg_d, eg = backward(pair, 0, 0, kept_d, *own_args, eg)
    hidden = hidden_gradient(eg, proj, proj_weight)
    from_x, hidden = lax.optimization_barrier((from_x, hidden))
    both = qg_d.astype(f32) + from_core[:2].astype(f32)
    for one in from_x:
        both = both + one.astype(f32)
    query_grad = reduce_y_z(both, order)
    return (query_grad, hidden.reshape(1, CAP, LEN, H))


def solution(mesh):
    return jax.shard_map(
        on_device,
        mesh=mesh,
        in_specs=(
            P("pb", None),
            P("pb", "pa", None, None),
            P(),
            P("pb", "pa", None),
            P("pb", "pa", None),
            P("pb", "pa"),
        ),
        out_specs=(P(("pb", "pa"), None), P("pb", "pa", None, None)),
        check_vma=False,
    )
```

```python
import functools
import math

import jax
import jax.numpy as jnp
from jax import lax
from jax.experimental import pallas as pl
from jax.experimental.pallas import tpu as pltpu
from jax.sharding import PartitionSpec as P

DIM = 128
H = 1024
QT = 32
LEN = 128
PD = 8
DEPTH = 100
CAP = 16
ROWS = CAP * LEN
GROUPS = 16
GR = 256
GQ = GR // QT

tau = 0.05
inv_temp = 20.0
rrf_offset = 60.0
norm_eps = 1e-06
log2_scale = inv_temp / math.log(2.0)

bf16 = jnp.bfloat16
f32 = jnp.float32
NT = (((1,), (1,)), ((), ()))
NN = (((1,), (0,)), ((), ()))
HIGH = lax.Precision.HIGHEST


def swap(value, axis, mask):
    return lax.ppermute(value, axis, [(i, i ^ mask) for i in range(16)])


def shift_x(value, by):
    return lax.ppermute(
        value, "pb", [(i, ((((i >> 2) + by) % 4) << 2) | (i & 3)) for i in range(16)]
    )


SHIFTS = (0, 1, -1, 2)


def shift_z(value, by):
    return lax.ppermute(
        value, "pa", [(i, ((((i >> 1) + by) % 8) << 1) | (i & 1)) for i in range(16)]
    )


Z_PLACE = (0, 2, 7, 6, 4, 3, 5, 1)
Z_OFFSETS = (0, 1, 7, 3, 4, 2, 5, 6)


def swap_y(value, low, high):
    pairs = [(i, i ^ (32 * low + high)) for i in range(256)]
    return lax.ppermute(value, ("pb", "pa"), pairs)


def order_of(me):
    j = jnp.arange(16, dtype=jnp.int32)[:, None]
    offset = jnp.zeros_like(j)
    for place, one in enumerate(Z_OFFSETS):
        offset = jnp.where((j & 7) == place, one, offset)
    block = ((((me >> 1) + offset) & 7) << 1) + ((me & 1) ^ (j >> 3))
    return (block == jnp.arange(16, dtype=jnp.int32)[None, :]).astype(bf16)


def reduce_y_z(value, order):
    blocks = [
        lax.dot_general(
            order, rows.astype(bf16).reshape(16, 16 * DIM), NN, preferred_element_type=f32
        )
        .astype(bf16)
        .reshape(2, 8, 16, DIM)
        for rows in value
    ]
    got = [swap_y(blocks[1][1], 1, 1), swap_y(blocks[0][1], 0, 1), swap_y(blocks[1][0], 1, 0)]
    blocks = blocks[0][0].astype(f32)
    for one in got:
        blocks = blocks + one.astype(f32)
    up = shift_z(blocks[3:6].astype(bf16), 3).astype(f32)
    down = shift_z(blocks[6:].astype(bf16), -3).astype(f32)
    near_up = (blocks[1] + up[1] + down[1]).astype(bf16)
    near_down = (blocks[2] + up[2]).astype(bf16)
    up_one, down_one = shift_z(near_up, 1), shift_z(near_down, -1)
    return blocks[0] + up[0] + down[0] + up_one.astype(f32) + down_one.astype(f32)


def join_kernel(query_ref, first_ref, second_ref, out_ref):
    out_ref[:GR, :] = query_ref[...]
    ranks = jnp.concatenate([first_ref[...], second_ref[...]])
    out_ref[GR:, :] = ranks.astype(f32).astype(bf16)


def join(queries, bm25_rank, dense_rank):
    return pl.pallas_call(
        join_kernel,
        out_shape=jax.ShapeDtypeStruct((GR + 2 * GQ, DIM), bf16),
        compiler_params=pltpu.CompilerParams(vmem_limit_bytes=2 * 2**20),
        name="join",
    )(
        *(
            pltpu.with_memory_space_constraint(x, pltpu.HBM)
            for x in (queries, bm25_rank, dense_rank)
        )
    )


def project_kernel(hid_ref, w_ref, *rest):
    proj_ref, emb_ref, emb_t_ref = rest[-3:]
    proj = lax.dot_general(hid_ref[...], w_ref[...], NN, preferred_element_type=f32)
    scaling = lax.rsqrt(jnp.sum(proj * proj, axis=-1, keepdims=True) + norm_eps)
    unit = proj * scaling
    proj_ref[...] = proj
    emb_ref[...] = unit.astype(bf16)
    emb_t_ref[...] = unit.T.astype(bf16)


def project(hid, weight, half, made=(), after=()):
    step = ROWS // 2
    return pl.pallas_call(
        project_kernel,
        grid=(1,),
        in_specs=[
            pl.BlockSpec((step, H), lambda i: (half, 0)),
            pl.BlockSpec((H, DIM), lambda i: (0, 0)),
        ]
        + [pl.BlockSpec(memory_space=pl.ANY)] * (len(made) + len(after)),
        out_specs=[
            pl.BlockSpec((step, DIM), lambda i: (half, 0)),
            pl.BlockSpec((step, DIM), lambda i: (half, 0)),
            pl.BlockSpec((DIM, step), lambda i: (0, half)),
        ],
        out_shape=[
            jax.ShapeDtypeStruct((ROWS, DIM), f32),
            jax.ShapeDtypeStruct((ROWS, DIM), bf16),
            jax.ShapeDtypeStruct((DIM, ROWS), bf16),
        ],
        input_output_aliases={2 + i: i for i in range(len(made))},
        compiler_params=pltpu.CompilerParams(vmem_limit_bytes=12 * 2**20),
        cost_estimate=pl.CostEstimate(
            flops=ROWS * H * DIM // 4, bytes_accessed=ROWS * H // 4, transcendentals=0
        ),
        name="project",
    )(*(pltpu.with_memory_space_constraint(x, pltpu.HBM) for x in (hid, weight)), *made, *after)


def token_sums(value):
    high = value.astype(bf16)
    rest = value - high.astype(f32)
    middle = rest.astype(bf16)
    low = (rest - middle.astype(f32)).astype(bf16)
    row_q = lax.broadcasted_iota(jnp.int32, (GR, GR), 0) // QT
    col_q = lax.broadcasted_iota(jnp.int32, (GR, GR), 1) // QT
    same = (row_q == col_q).astype(f32).astype(bf16)
    parts = [lax.dot_general(v, same, NN, preferred_element_type=f32) for v in (high, middle, low)]
    return parts[0] + (parts[1] + parts[2])


def forward_kernel(q_ref, emb_ref, *rest):
    p_ref, lse_ref, total_ref = rest[-3:]
    queries = q_ref[0, :GR, :]
    tops, sums = [], []
    for k in range(CAP):
        rows = slice(k * LEN, (k + 1) * LEN)
        raw = lax.dot_general(emb_ref[rows, :], queries, NT, preferred_element_type=f32)
        top = jnp.max(raw, axis=0, keepdims=True)
        p = jnp.exp2((raw - top) * log2_scale)
        p_ref[0, rows, :] = p.astype(bf16)
        tops.append(top)
        sums.append(jnp.sum(p, axis=0, keepdims=True))
    top = jnp.concatenate(tops, axis=0)
    total = jnp.concatenate(sums, axis=0)
    lse_ref[0] = inv_temp * top + jnp.log(total)
    total_ref[0] = total


def forward(gathered, start, count, emb, place, size, kept=(), after=()):
    height = gathered.shape[1]
    step = lambda g: (g + place, 0, 0)
    return pl.pallas_call(
        forward_kernel,
        grid=(count,),
        in_specs=[
            pl.BlockSpec((1, height, DIM), lambda g: (g + start, 0, 0)),
            pl.BlockSpec((ROWS, DIM), lambda g: (0, 0)),
        ]
        + [pl.BlockSpec(memory_space=pl.ANY)] * (len(kept) + len(after)),
        out_specs=[
            pl.BlockSpec((1, ROWS, GR), step),
            pl.BlockSpec((1, CAP, GR), step),
            pl.BlockSpec((1, CAP, GR), step),
        ],
        out_shape=[
            jax.ShapeDtypeStruct((size, ROWS, GR), bf16),
            jax.ShapeDtypeStruct((size, CAP, GR), f32),
            jax.ShapeDtypeStruct((size, CAP, GR), f32),
        ],
        input_output_aliases={2 + i: i for i in range(len(kept))},
        compiler_params=pltpu.CompilerParams(vmem_limit_bytes=6 * 2**20),
        cost_estimate=pl.CostEstimate(
            flops=2 * count * GR * ROWS * DIM // 4,
            bytes_accessed=count * 2 * GR * ROWS // 4,
            transcendentals=count * GR * ROWS // 4,
        ),
        name="forward",
    )(gathered, emb, *kept, *after)


def backward_kernel(
    first, half, q_at, q_ref, p_ref, lse_ref, total_ref, emb_t_ref, pick_ref, *rest
):
    target_refs = rest[:3]
    qg_ref, eg_ref, c_ref, own_ref, score_ref = rest[-5:]
    g = pl.program_id(0)

    @pl.when(g == 0)
    def _():
        eg_ref[...] = jnp.zeros_like(eg_ref) if first else rest[3][...]
        own = jnp.zeros((CAP, LEN), f32)
        for j in range(3):
            part = target_refs[j][:, :, half * LEN : (half + 1) * LEN].reshape(6 * PD, LEN)
            own += lax.dot_general(
                pick_ref[j], part, NN, precision=HIGH, preferred_element_type=f32
            )
        own_ref[...] = own
        score = token_sums(lse_ref[...].reshape(-1, GR)) * (tau / QT)
        score_ref[...] = score.reshape(score_ref.shape)

    queries = q_ref[:, :GR, :].reshape(2 * GR, DIM)
    pick = pick_ref[...]
    held = jnp.sum(pick[0] + pick[1] + pick[2], axis=1, keepdims=True)
    own = own_ref[...]
    lane = lax.broadcasted_iota(jnp.int32, (CAP, LEN), 1) // QT
    for u in range(2):
        factors = []
        for k in range(2):
            lanes = slice(k * LEN, (k + 1) * LEN)
            at = lane + ((2 * g + u + q_at) * 2 * GQ + k * (GQ // 2))
            target = jnp.take_along_axis(own, at, axis=1, mode="promise_in_bounds")
            residual = (score_ref[2 * g + u, :, lanes] - target).astype(bf16).astype(f32) * held
            factors.append((residual / QT) / total_ref[u, :, lanes])
        factor = jnp.concatenate(factors, axis=1)
        for k in range(CAP):
            rows = slice(k * LEN, (k + 1) * LEN)
            c_ref[rows, u * GR : (u + 1) * GR] = (
                p_ref[u, rows, :].astype(f32) * factor[k : k + 1, :]
            ).astype(bf16)
    eg_ref[...] += lax.dot_general(c_ref[...], queries, NN, preferred_element_type=f32)
    qg = lax.dot_general(emb_t_ref[...], c_ref[...], NN, preferred_element_type=f32)
    qg_ref[...] = qg.T.astype(bf16).reshape(2, GR, DIM)


def backward(gathered, start, half, kept, emb_t, pick, targets, emb_grad=None):
    height = gathered.shape[1]
    p, lse, total = kept
    count = p.shape[0]
    first = emb_grad is None
    whole = lambda g: (0, 0)
    step = lambda g: (g, 0, 0)
    fixed = lambda g: (0, 0, 0)
    in_specs = [
        pl.BlockSpec((2, height, DIM), lambda g: (g + start // 2, 0, 0)),
        pl.BlockSpec((2, ROWS, GR), step),
        pl.BlockSpec((count, CAP, GR), fixed),
        pl.BlockSpec((2, CAP, GR), step),
        pl.BlockSpec((DIM, ROWS), whole),
        pl.BlockSpec((3, CAP, 6 * PD), fixed),
    ] + [pl.BlockSpec((6, PD, 2 * LEN), fixed)] * 3
    args = [gathered, p, lse, total, emb_t, pick, *targets]
    if not first:
        in_specs.append(pl.BlockSpec((ROWS, DIM), whole))
        args.append(emb_grad)
    return pl.pallas_call(
        functools.partial(backward_kernel, first, half, start),
        grid=(count // 2,),
        in_specs=in_specs,
        out_specs=[pl.BlockSpec((2, GR, DIM), step), pl.BlockSpec((ROWS, DIM), whole)],
        out_shape=[
            jax.ShapeDtypeStruct((count, GR, DIM), bf16),
            jax.ShapeDtypeStruct((ROWS, DIM), f32),
        ],
        scratch_shapes=[
            pltpu.VMEM((ROWS, 2 * GR), bf16),
            pltpu.VMEM((CAP, LEN), f32),
            pltpu.VMEM((count, CAP, GR), f32),
        ],
        compiler_params=pltpu.CompilerParams(vmem_limit_bytes=14 * 2**20),
        cost_estimate=pl.CostEstimate(
            flops=4 * count * GR * ROWS * DIM,
            bytes_accessed=count * 2 * GR * ROWS,
            transcendentals=0,
        ),
        name="backward",
    )(*args)


def hidden_kernel(eg_ref, proj_ref, w_ref, out_ref):
    proj = proj_ref[...]
    scaling = lax.rsqrt(jnp.sum(proj * proj, axis=-1, keepdims=True) + norm_eps)
    unit = proj * scaling
    slot_grad = eg_ref[...].astype(bf16).astype(f32)
    inner = jnp.sum(unit * slot_grad, axis=-1, keepdims=True)
    proj_grad = ((slot_grad - unit * inner) * scaling).astype(bf16)
    out_ref[...] = lax.dot_general(
        proj_grad, w_ref[...], NT, preferred_element_type=f32
    ).astype(bf16)


def hidden_gradient(emb_grad, proj, weight):
    step = 1024
    return pl.pallas_call(
        hidden_kernel,
        grid=(ROWS // step,),
        in_specs=[
            pl.BlockSpec((step, DIM), lambda i: (i, 0)),
            pl.BlockSpec((step, DIM), lambda i: (i, 0)),
            pl.BlockSpec((H, DIM), lambda i: (0, 0)),
        ],
        out_specs=pl.BlockSpec((step, H), lambda i: (i, 0)),
        out_shape=jax.ShapeDtypeStruct((ROWS, H), bf16),
        compiler_params=pltpu.CompilerParams(vmem_limit_bytes=12 * 2**20),
        cost_estimate=pl.CostEstimate(
            flops=2 * ROWS * H * DIM, bytes_accessed=ROWS * (2 * H + 8 * DIM), transcendentals=0
        ),
        name="hidden_gradient",
    )(emb_grad, proj, weight)


def target_kernel(first_ref, near_ref, far_ref, out_ref):
    row = lax.broadcasted_iota(jnp.int32, (2 * PD, LEN), 0) + first_ref[0]
    own = (row == lax.broadcasted_iota(jnp.int32, (2 * PD, LEN), 1)).astype(f32).astype(bf16)
    for half, ref in enumerate((near_ref, far_ref)):
        ranks = ref[...].reshape(LEN, LEN)
        rank = lax.dot_general(own, ranks, NT, preferred_element_type=f32)[:PD]
        term = rank_term(rank)
        out_ref[:, half * LEN : (half + 1) * LEN] = term + pltpu.roll(term, LEN - GQ, 1)


def targets_of(first_row, near, far):
    rows = pl.BlockSpec((8, 2 * GQ, DIM), lambda i: (0, GR // (2 * GQ), 0))
    return pl.pallas_call(
        target_kernel,
        grid=(1,),
        in_specs=[pl.BlockSpec(memory_space=pltpu.SMEM), rows, rows],
        out_specs=pl.BlockSpec((PD, 2 * LEN), lambda i: (0, 0)),
        out_shape=jax.ShapeDtypeStruct((PD, 2 * LEN), f32),
        compiler_params=pltpu.CompilerParams(vmem_limit_bytes=2 * 2**20),
        name="targets",
    )(first_row, near, far)


def rank_term(rank):
    return jnp.where(rank < DEPTH, rrf_offset / (rrf_offset + rank), 0.0)


def on_device(
    queries, encoder_outputs, proj_weight, bm25_rank, dense_rank, custodian_document_index
):
    me_pb, me_pa = lax.axis_index("pb"), lax.axis_index("pa")
    slot_ids = custodian_document_index[0]
    shard = slot_ids >> 3
    offset = ((shard >> 1) - (me_pa >> 1)) & 7
    place = jnp.zeros_like(offset)
    for at, one in enumerate(Z_PLACE):
        place = jnp.where(offset == at, one, place)
    place = (place * 2 + ((shard ^ me_pa) & 1)) * PD + (slot_ids & 7)
    place = jnp.where(slot_ids >= 0, place, -1)
    rows = jnp.arange(18 * PD, dtype=jnp.int32).reshape(3, 1, 6 * PD)
    pick = (place[None, :, None] == rows).astype(f32)
    mine = join(queries, bm25_rank[:, 0, :], dense_rank[:, 0, :])
    other = swap(mine, "pb", 2)
    first_row, order = (me_pb * PD).reshape(1), order_of(me_pa)
    hid = encoder_outputs.reshape(ROWS, H)
    made = project(hid, proj_weight, 0, after=[mine])
    other, pick, order, first_row = lax.optimization_barrier((other, pick, order, first_row))
    pair = jnp.stack([mine, other])
    proj, emb, emb_t = project(hid, proj_weight, 1, made, [pair])
    got = [shift_x(pair, by) for by in SHIFTS[1:]]
    kept_d = forward(pair, 0, 2, emb, 0, 2)
    got, kept_d = lax.optimization_barrier((got, kept_d))
    plane = jnp.concatenate([pair] + got)
    far = swap(plane, "pb", 1)
    kept_b = forward(plane, 2, 4, emb, 0, 6)
    far, kept_b = lax.optimization_barrier((far, kept_b))
    target = targets_of(first_row, plane, far)
    from_y = swap(target, "pa", 1)
    kept_b = forward(plane, 6, 2, emb, 4, 6, kept_b, [target])
    kept_f = forward(far, 0, 2, emb, 0, 8, after=[target])
    from_y, kept_b, kept_f = lax.optimization_barrier((from_y, kept_b, kept_f))
    targets = jnp.stack([target, from_y])
    from_z = [shift_z(targets, 1), shift_z(targets, -1)]
    kept_f = forward(far, 2, 2, emb, 2, 8, kept_f)
    from_z, kept_f = lax.optimization_barrier((from_z, kept_f))
    targets = jnp.concatenate([targets] + from_z)
    from_z = [shift_z(targets, 3), shift_z(targets, -3)]
    kept_f = forward(far, 4, 4, emb, 4, 8, kept_f)
    from_z, kept_f = lax.optimization_barrier((from_z, kept_f))
    own_args = (emb_t, pick, [targets] + from_z)
    qg_f, eg = backward(far, 0, 1, kept_f, *own_args)
    from_core = swap(qg_f, "pb", 1)
    qg_b, eg = backward(plane, 2, 0, kept_b, *own_args, eg)
    sent = (qg_b.astype(f32) + from_core[2:].astype(f32)).astype(bf16).reshape(3, 2, GR, DIM)
    from_x = [shift_x(sent[a - 1], -SHIFTS[a]) for a in (1, 2, 3)]
    qg_d, eg = backward(pair, 0, 0, kept_d, *own_args, eg)
    hidden = hidden_gradient(eg, proj, proj_weight)
    from_x, hidden = lax.optimization_barrier((from_x, hidden))
    both = qg_d.astype(f32) + from_core[:2].astype(f32)
    for one in from_x:
        both = both + one.astype(f32)
    query_grad = reduce_y_z(both, order)
    return (query_grad, hidden.reshape(1, CAP, LEN, H))


def solution(mesh):
    return jax.shard_map(
        on_device,
        mesh=mesh,
        in_specs=(
            P("pb", None),
            P("pb", "pa", None, None),
            P(),
            P("pb", "pa", None),
            P("pb", "pa", None),
            P("pb", "pa"),
        ),
        out_specs=(P(("pb", "pa"), None), P("pb", "pa", None, None)),
        check_vma=False,
    )
```
